256 devices in a mesh: cache: 32 (over y, z), tp: 8 (over x, core).
Axes of the slice: x: 4, y: 4, z: 8, core: 2. Of those that a mesh axis runs over, the one named last changes fastest.
Arguments:
- conv_input: bfloat16 [2, 64, 256, 8, 768], P(None, 'cache', None, 'tp'), may hold values from -6 to 6
- conv_weight: bfloat16 [2, 4, 8, 768], P(None, None, 'tp'), may hold values from -3 to 3
- conv_bias: float32 [2, 8, 768], P(None, 'tp'), may hold values from -3 to 3
- step_raw: bfloat16 [2, 64, 64, 256], P(None, 'cache', 'tp'), may hold values from -1.5 to 1.5
- step_bias: float32 [2, 64], P(None, 'tp'), may hold values from -3.5 to -2.5
- decay_log: float32 [2, 64], P(None, 'tp'), may hold values from -3.5 to -0.5
- skip_weight: float32 [2, 64], P(None, 'tp'), may hold values from 0.5 to 1.5
- gate_input: bfloat16 [2, 64, 256, 4096], P(None, 'cache', None, 'tp'), may hold values from -6 to 6
- norm_gain: float32 [2, 4096], P(None, 'tp'), may hold values from 0.25 to 1.75
- out_weight: bfloat16 [2, 4096, 2048], P(None, 'tp'), may hold values from -0.09375 to 0.09375
- ssm_state: bfloat16 [2, 64, 64, 64, 128], P(None, 'cache', 'tp'), may hold values from -1.1953125 to 1.1953125
- conv_state: bfloat16 [2, 64, 3, 8, 768], P(None, 'cache', None, 'tp'), may hold values from -6 to 6
- pool_ssm: bfloat16 [512, 64, 64, 128], P('cache', 'tp'), may hold values from -1.1953125 to 1.1953125
- pool_conv: bfloat16 [512, 3, 8, 768], P('cache', None, 'tp'), may hold values from -6 to 6
- lengths: int32 [64], P('cache'), may hold values from 1 to 256
- store_offset: int32 [64, 8, 1], replicated, may hold values from 0 to 3; in each aligned block of 16 rows (0 to 15, 16 to 31, ..., all dimensions but the last counted through in order) at most 8 rows name the same one
- store_base: int32 [32], P('cache'), may hold values from 0 to 15
- hit_offset: int32 [64, 2, 1], replicated, may hold values from 0 to 3; in each aligned block of 4 rows (0 to 3, 4 to 7, ..., all dimensions but the last counted through in order) at most 2 rows name the same one
- hit_row: int32 [64, 2], replicated, may hold values from 0 to 15
Outputs:
- mixed_rows: bfloat16 [2, 64, 256, 2048], P(None, 'cache', None, 'tp')
- pool_ssm_out: bfloat16 [512, 64, 64, 128], P('cache', 'tp')
- pool_conv_out: bfloat16 [512, 3, 8, 768], P('cache', None, 'tp')
- next_ssm: bfloat16 [2, 64, 64, 64, 128], P(None, 'cache', 'tp')
- next_conv: bfloat16 [2, 64, 3, 8, 768], P(None, 'cache', None, 'tp')
The draws below stay inside these ranges and needn't reach their ends.
Inputs may be any that keep to these rules, and one draw needn't show every extreme that they name: `store_offset`: within the rows of one device (aligned blocks of 16 entries), no offset appears more than 8 times, and in some block one appears exactly 8 times. `hit_offset`: within the rows of one device (aligned blocks of 4 entries), no offset appears more than 2 times, and in some block one appears exactly 2 times.
All inputs are finite; a program needn't handle non-finite values.
Results may differ from the reference program's by a relative error of at most 0.017.
Values may be sent and summed in bfloat16 or wider, within the bound.
No kernel may reach another device: no remote copies, remote signals or barrier semaphores. Data moves between devices by JAX's collectives and lax.ppermute only.
A program may use at most 128 MiB of HBM per device.

```python
import math
import jax
import jax.numpy as jnp
import numpy as np
from jax import lax

HEADS = 64
HEAD_DIM = 64
STATE = 128
GROUPS = 8
CONV_K = 4
SPAN = 256
DOUT = 2048
LAYERS = 2
BOUNDS = 4
WINDOW = 4
SLOT_DEV = 2
PAIR_MOST = 8
HIT_MOST = 2
ROWS_DEV = 16
SLOTS = 64
INNER = 4096
GROUP_WIDTH = 768
N_CACHE = 32
N_TP = 8


def draw_decay_log(key, part):
    key = jax.random.fold_in(key, 11)
    return jax.random.uniform(key, (LAYERS, HEADS), jnp.float32, -3.5, -0.5)


def plant(array, key, smallest, largest):
    longest = array.shape.index(max(array.shape))
    spots = []
    for shift in (0, 1):
        where = [jax.random.randint(jax.random.fold_in(key, axis), (), 0, length) for axis, length in enumerate(array.shape)]
        where[longest] = (where[longest] + shift) % array.shape[longest]
        spots.append(tuple(where))
    return array.at[spots[0]].set(smallest).at[spots[1]].set(largest)


def shard_levels(rng, dims, pieces, least, largest):
    loudness, own = 1.0, jax.random.fold_in(rng, 6)
    for axis_at, blocks in pieces:
        draws = jnp.exp(jax.random.uniform(jax.random.fold_in(own, axis_at), (blocks,), jnp.float32, least / len(pieces), largest / len(pieces)))
        loudness = loudness * jnp.repeat(draws, dims[axis_at] // blocks).reshape([-1 if axis == axis_at else 1 for axis in range(len(dims))])
    return loudness


def shared_out(stream_key, own, number, rows, number_of, top, reach, skew):
    order = jax.random.permutation(stream_key, number_of)
    crowded, common = shares(number_of, rows * top, reach, skew, True), shares(number_of, rows * top, reach, skew, False)
    places = jnp.arange(number_of)

    def named(sizes, rotation):
        used = int((sizes > 0).sum())
        fixed = max(1, used // 4)
        shifted = fixed + (places - fixed + rotation * (used - fixed)) % max(1, number_of - fixed)
        return jnp.zeros((number_of,), jnp.int32).at[order[jnp.where(places < fixed, places, shifted)]].set(jnp.asarray(sizes, jnp.int32))

    sizes = jnp.where(number % 4 == 0, named(crowded, number // 4), named(common, number - number // 4 - 1))
    mixed = jax.random.permutation(jax.random.fold_in(own, 3), number_of)
    donor, taker = mixed[0:number_of // 2 * 2:2], mixed[1:number_of // 2 * 2:2]
    slack = jnp.minimum(sizes[donor] - 1, reach - sizes[taker]) // 2
    slack = jnp.where((donor == order[0]) | (taker == order[0]) | (sizes[taker] == 0), 0, jnp.maximum(slack, 0))
    shifted = jax.random.randint(jax.random.fold_in(own, 4), (number_of // 2,), 0, 1 << 20) % (slack + 1)
    sizes = sizes.at[donor].add(-shifted).at[taker].add(shifted)
    labels = jnp.searchsorted(jnp.cumsum(sizes), jnp.arange(rows * top), side="right").astype(jnp.int32)
    grid = labels.reshape(top, rows).T
    grid = grid[jax.random.permutation(jax.random.fold_in(own, 1), rows)]
    rotation = jax.random.randint(jax.random.fold_in(own, 2), (rows, 1), 0, top)
    return jnp.take_along_axis(grid, (jnp.arange(top)[None, :] + rotation) % top, axis=1)


def shares(amount, total, reach, slope, full):
    loads = [(1 << 20) // math.isqrt(grade ** slope) + 1 for grade in range(1, amount + 1)]
    largest = reach if full else min(reach, max(-(-total // amount), total * loads[0] // sum(loads)))
    least = 1 if total - largest >= amount - 1 else 0
    holding, spare = [largest] + [least] * (amount - 1), total - largest - least * (amount - 1)
    while spare > 0:
        movable = [i for i in range(1, amount) if holding[i] < largest] or [i for i in range(1, amount) if holding[i] < reach]
        pool, budget = sum([loads[i] for i in movable]), spare
        for i in movable:
            more = min(reach - holding[i], max(1, budget * loads[i] // pool), spare)
            holding[i] = holding[i] + more
            spare = spare - more
    return np.array(holding)


def scatter_about(rng, dims, deviation, most, cuts=(), kind=jnp.bfloat16):
    drawn = jax.random.normal(rng, dims, jnp.float32) * deviation
    if len(cuts) > 0:
        drawn = shard_levels(rng, dims, cuts, -0.22, 0.18) * drawn
    return jnp.clip(drawn, min=-most, max=most).astype(kind)


def setup_inputs(seed: int = 0) -> dict:
    streams_of = jax.random.split(jax.random.key(seed), 20)
    conv_input = scatter_about(streams_of[0], (LAYERS, SLOTS, SPAN, GROUPS, GROUP_WIDTH), 1.0, 6.0, ((1, 32), (3, 8)))
    conv_weight = scatter_about(streams_of[1], (LAYERS, CONV_K, GROUPS, GROUP_WIDTH), CONV_K ** -0.5, 3.0, ((2, 8),))
    conv_bias = scatter_about(streams_of[2], (LAYERS, GROUPS, GROUP_WIDTH), 0.5, 3.0, ((1, 8),), jnp.float32)
    step_raw = scatter_about(streams_of[3], (LAYERS, SLOTS, HEADS, SPAN), 0.5, 1.5, ((1, 32), (2, 8)))
    step_bias = jnp.clip(-3.5 + 1.0 * jax.random.uniform(streams_of[4], (LAYERS, HEADS), jnp.float32) ** shard_levels(streams_of[4], (LAYERS, HEADS), ((1, 8),), -0.2, 0.2), -3.5, -2.5)
    decay_log = draw_decay_log(jax.random.fold_in(streams_of[19], 71), 0)
    skip_weight = jnp.clip(0.5 + 1.0 * jax.random.uniform(streams_of[6], (LAYERS, HEADS), jnp.float32) ** shard_levels(streams_of[6], (LAYERS, HEADS), ((1, 8),), -0.2, 0.2), 0.5, 1.5)
    gate_input = scatter_about(streams_of[7], (LAYERS, SLOTS, SPAN, INNER), 1.0, 6.0, ((1, 32), (3, 8)))
    norm_gain = jnp.clip(1.0 + 0.15 * jax.random.normal(streams_of[8], (LAYERS, INNER), jnp.float32), 0.25, 1.75)
    out_weight = scatter_about(streams_of[9], (LAYERS, INNER, DOUT), INNER ** -0.5, 0.09375, ((1, 8),))
    ssm_state = scatter_about(streams_of[10], (LAYERS, SLOTS, HEADS, HEAD_DIM, STATE), 0.2, 1.1953125, ((1, 32), (2, 8)))
    conv_state = scatter_about(streams_of[11], (LAYERS, SLOTS, CONV_K - 1, GROUPS, GROUP_WIDTH), 1.0, 6.0, ((1, 32), (3, 8)))
    pool_ssm = scatter_about(streams_of[12], (N_CACHE * ROWS_DEV, HEADS, HEAD_DIM, STATE), 0.2, 1.1953125, ((0, 32), (1, 8)))
    pool_conv = scatter_about(streams_of[13], (N_CACHE * ROWS_DEV, CONV_K - 1, GROUPS, GROUP_WIDTH), 1.0, 6.0, ((0, 32), (2, 8)))
    lengths = plant(jax.random.randint(streams_of[14], (SLOTS,), 1, SPAN + 1), jax.random.fold_in(streams_of[14], 1), 1, SPAN).astype(jnp.int32)
    store_offset_keys = jax.random.split(jax.random.fold_in(streams_of[15], 1), SLOTS * (LAYERS * BOUNDS) // (SLOT_DEV * LAYERS * BOUNDS))
    store_offset_turns = jax.random.permutation(jax.random.fold_in(streams_of[15], 3), SLOTS * (LAYERS * BOUNDS) // (SLOT_DEV * LAYERS * BOUNDS))
    store_offset = jax.vmap(lambda own, number: shared_out(jax.random.fold_in(streams_of[15], 2), own, number, SLOT_DEV * LAYERS * BOUNDS, WINDOW, 1, PAIR_MOST, 2))(store_offset_keys, store_offset_turns).reshape((SLOTS, LAYERS * BOUNDS, 1))
    store_base = plant(jax.random.randint(streams_of[16], (N_CACHE,), 0, ROWS_DEV), jax.random.fold_in(streams_of[16], 1), 0, ROWS_DEV - 1).astype(jnp.int32)
    hit_offset_keys = jax.random.split(jax.random.fold_in(streams_of[17], 1), SLOTS * LAYERS // (SLOT_DEV * LAYERS))
    hit_offset_turns = jax.random.permutation(jax.random.fold_in(streams_of[17], 3), SLOTS * LAYERS // (SLOT_DEV * LAYERS))
    hit_offset = jax.vmap(lambda own, number: shared_out(jax.random.fold_in(streams_of[17], 2), own, number, SLOT_DEV * LAYERS, WINDOW, 1, HIT_MOST, 1))(hit_offset_keys, hit_offset_turns).reshape((SLOTS, LAYERS, 1))
    hit_row = plant(jax.random.randint(streams_of[18], (SLOTS, LAYERS), 0, ROWS_DEV), jax.random.fold_in(streams_of[18], 1), 0, ROWS_DEV - 1).astype(jnp.int32)
    return {"conv_input": conv_input, "conv_weight": conv_weight, "conv_bias": conv_bias, "step_raw": step_raw, "step_bias": step_bias, "decay_log": decay_log, "skip_weight": skip_weight, "gate_input": gate_input, "norm_gain": norm_gain, "out_weight": out_weight, "ssm_state": ssm_state, "conv_state": conv_state, "pool_ssm": pool_ssm, "pool_conv": pool_conv, "lengths": lengths, "store_offset": store_offset, "store_base": store_base, "hit_offset": hit_offset, "hit_row": hit_row}


EPS = 1e-05

def mixer_slot(conv_in, conv_taps, conv_shift, step_in, step_bias, decay_log, skip_weight, gate_rows, gain_row, state_init, conv_init, seq_length):
    span_len = conv_in.shape[0]
    per_group = HEADS // GROUPS
    inner_group = per_group * HEAD_DIM
    extended = jnp.concatenate([conv_init, conv_in], axis=0)
    summed = conv_shift.astype(jnp.float32)[None]
    for position in range(CONV_K):
        summed = summed + conv_taps[position].astype(jnp.float32)[None] * extended[position:position + span_len].astype(jnp.float32)
    active = jax.nn.silu(summed).astype(jnp.bfloat16)
    x_heads = active[:, :, :inner_group].reshape(span_len, HEADS, HEAD_DIM)
    b_rows = active[:, :, inner_group:inner_group + STATE]
    c_rows = active[:, :, inner_group + STATE:]
    valid_rows = jnp.arange(span_len) < seq_length
    step_size = jax.nn.softplus(step_in.astype(jnp.float32) + step_bias[:, None]) * valid_rows[None, :].astype(jnp.float32)
    cumulative = jnp.cumsum(step_size * (-jnp.exp(decay_log))[:, None], axis=1)
    scores = jnp.einsum('tgn,ugn->gtu', c_rows.astype(jnp.float32), b_rows.astype(jnp.float32))
    head_scores = jnp.repeat(scores, per_group, axis=0)
    causal = jnp.arange(span_len)[:, None] >= jnp.arange(span_len)[None, :]
    difference = cumulative[:, :, None] - cumulative[:, None, :]
    decay_mask = jnp.where(causal[None], jnp.exp(jnp.where(causal[None], difference, 0.0)), 0.0)
    weights = (head_scores * decay_mask * step_size[:, None, :]).astype(jnp.bfloat16)
    diag_out = jnp.einsum('htu,uhp->thp', weights.astype(jnp.float32), x_heads.astype(jnp.float32))
    c_heads = jnp.repeat(c_rows, per_group, axis=1)
    carried = jnp.einsum('thn,hpn->thp', c_heads.astype(jnp.float32), state_init.astype(jnp.float32))
    output = diag_out + carried * jnp.exp(cumulative).T[:, :, None] + skip_weight[None, :, None] * x_heads.astype(jnp.float32)
    block_len = span_len // BOUNDS
    ends = (jnp.arange(BOUNDS, dtype=jnp.int32) + 1) * block_len - 1
    end_cum = cumulative.reshape(HEADS, BOUNDS, block_len)[:, :, -1]
    upto = jnp.arange(span_len, dtype=jnp.int32)[None, :] <= ends[:, None]
    gap = end_cum.T[:, :, None] - cumulative[None]
    tail_weight = jnp.where(upto[:, None, :], jnp.exp(jnp.where(upto[:, None, :], gap, 0.0)), 0.0) * step_size[None]
    weighted = (x_heads.astype(jnp.float32)[None] * jnp.transpose(tail_weight, (0, 2, 1))[:, :, :, None]).astype(jnp.bfloat16)
    b_heads = jnp.repeat(b_rows, per_group, axis=1)
    new_states = jnp.einsum('kthp,thn->khpn', weighted.astype(jnp.float32), b_heads.astype(jnp.float32))
    new_states = (new_states + jnp.exp(end_cum).T[:, :, None, None] * state_init.astype(jnp.float32)[None]).astype(jnp.bfloat16)
    gated_out = output.reshape(span_len, HEADS * HEAD_DIM) * jax.nn.silu(gate_rows.astype(jnp.float32))
    grouped = gated_out.reshape(span_len, GROUPS, inner_group)
    inverse_rms = lax.rsqrt(lax.optimization_barrier(jnp.mean(grouped * grouped, axis=-1, keepdims=True)) + EPS)
    normed = (grouped * inverse_rms).reshape(span_len, HEADS * HEAD_DIM) * gain_row[None, :]
    normed = jnp.where(valid_rows[:, None], normed, 0.0).astype(jnp.bfloat16)
    starts = jnp.minimum(seq_length.astype(jnp.int32), ends + 1).astype(jnp.int32)
    conv_tails = jnp.stack([lax.dynamic_slice_in_dim(extended, starts[bound], CONV_K - 1, 0) for bound in range(BOUNDS)], axis=0)
    return (normed, new_states, conv_tails)

def reference(conv_input, conv_weight, conv_bias, step_raw, step_bias, decay_log, skip_weight, gate_input, norm_gain, out_weight, ssm_state, conv_state, pool_ssm, pool_conv, lengths, store_offset, store_base, hit_offset, hit_row):
    mixed_list = []
    state_list = []
    tail_list = []
    block_inner = HEADS * HEAD_DIM // N_TP
    for layer_index in range(LAYERS):

        def run_slot(packed, layer_index=layer_index):
            conv_in, step_in, gate_rows, state_init, conv_init, seq_length = packed
            return mixer_slot(conv_in, conv_weight[layer_index], conv_bias[layer_index], step_in, step_bias[layer_index], decay_log[layer_index], skip_weight[layer_index], gate_rows, norm_gain[layer_index], state_init, conv_init, seq_length)
        normed, new_states, conv_tails = lax.map(run_slot, (conv_input[layer_index], step_raw[layer_index], gate_input[layer_index], ssm_state[layer_index], conv_state[layer_index], lengths))
        flat_rows = normed.reshape(SLOTS * SPAN, HEADS * HEAD_DIM)
        projected = jnp.zeros((SLOTS * SPAN, DOUT), jnp.float32)
        for block in range(N_TP):
            part = jnp.dot(flat_rows[:, block * block_inner:(block + 1) * block_inner], out_weight[layer_index, block * block_inner:(block + 1) * block_inner], preferred_element_type=jnp.float32).astype(jnp.bfloat16)
            part = lax.optimization_barrier(part)
            projected = projected + part.astype(jnp.float32)
        mixed_list.append(projected.astype(jnp.bfloat16).reshape(SLOTS, SPAN, DOUT))
        state_list.append(new_states)
        tail_list.append(conv_tails)
    mixed_rows = jnp.stack(mixed_list, axis=0)
    item_count = SLOTS * LAYERS * BOUNDS
    item_order = jnp.arange(item_count, dtype=jnp.int32)
    home = item_order // (LAYERS * BOUNDS) // SLOT_DEV
    owner_list = ((home + store_offset.reshape(item_count).astype(jnp.int32)) % N_CACHE).astype(jnp.int32)
    same_owner = owner_list[:, None] == owner_list[None, :]
    earlier = item_order[None, :] < item_order[:, None]
    rank_all = lax.optimization_barrier(jnp.sum(same_owner & earlier, axis=1)).astype(jnp.int32)
    cycle_base = store_base[owner_list].astype(jnp.int32)
    target_row = jnp.where(rank_all < ROWS_DEV, owner_list * ROWS_DEV + (cycle_base + rank_all) % ROWS_DEV, N_CACHE * ROWS_DEV).astype(jnp.int32)
    items_ssm = jnp.stack(state_list, axis=1).reshape(item_count, HEADS, HEAD_DIM, STATE)
    items_conv = jnp.stack(tail_list, axis=1).reshape(item_count, CONV_K - 1, GROUPS, GROUP_WIDTH)
    pool_ssm_out = pool_ssm.at[target_row].set(items_ssm, mode='drop')
    pool_conv_out = pool_conv.at[target_row].set(items_conv, mode='drop')
    hit_count = SLOTS * LAYERS
    hit_order = jnp.arange(hit_count, dtype=jnp.int32)
    hit_home = hit_order // LAYERS // SLOT_DEV
    hit_owner = (hit_home + hit_offset.reshape(hit_count).astype(jnp.int32)) % N_CACHE
    hit_flat = (hit_owner * ROWS_DEV + hit_row.reshape(hit_count).astype(jnp.int32)).astype(jnp.int32)
    next_ssm = jnp.transpose(pool_ssm_out[hit_flat].reshape(SLOTS, LAYERS, HEADS, HEAD_DIM, STATE), (1, 0, 2, 3, 4))
    next_conv = jnp.transpose(pool_conv_out[hit_flat].reshape(SLOTS, LAYERS, CONV_K - 1, GROUPS, GROUP_WIDTH), (1, 0, 2, 3, 4))
    return (mixed_rows, pool_ssm_out, pool_conv_out, next_ssm, next_conv)
```

```python
import functools

import jax
import jax.numpy as jnp
from jax import lax
from jax.experimental import pallas as pl
from jax.experimental.pallas import tpu as pltpu
from jax.sharding import PartitionSpec as P

BOUNDS = 4
WINDOW = 4
EPS = 1e-05
STATE_ROWS = 512
ITEM_ROWS = 544
TAIL_ROWS = 32
ITEMS = 16
VMEM_BYTES = 60 * 2**20
F32 = jnp.float32
BF16 = jnp.bfloat16
CUTS = (0, 8, 12, 14, 16)
SIZES = tuple(end - begin for begin, end in zip(CUTS, CUTS[1:]))
DOWN = (4, 4, 2)


def passed_along(array, by):
    size = lax.axis_size("cache")
    return lax.ppermute(array, "cache", [(i, (i + by) % size) for i in range(size)])


def silu(v):
    return 0.5 * v * (1.0 + jnp.tanh(0.5 * v))


def states_kernel(
    me_ref,
    offset_ref,
    length_ref,
    bias_ref,
    decay_ref,
    offsets_ref,
    conv_in_ref,
    conv_state_ref,
    taps_ref,
    shift_ref,
    step_ref,
    init_ref,
    active_ref,
    cum_ref,
    size_ref,
    more_ref,
    *refs,
):
    pieces = refs[: len(SIZES)]
    ext, tail, held, sems = refs[len(SIZES) :]
    turn = pl.program_id(0)

    @pl.when(turn == 0)
    def _():
        offsets = offsets_ref[...]
        even = lax.broadcasted_iota(jnp.int32, (1, 64), 1) % 2 == 0
        more = jnp.zeros((1, 64), jnp.bool_)
        for n, most in ((1, CUTS[3]), (2, CUTS[2])):
            of_slot = jnp.sum(jnp.where(offsets >= n, 1.0, 0.0), axis=0, keepdims=True)
            after_it = jnp.concatenate([of_slot[:, 1:], of_slot[:, :1]], axis=1)
            more = more | (even & (of_slot + after_it > most))
        more_ref[0] = jnp.max(jnp.where(more, 1.0, 0.0)).astype(jnp.int32)

    slot, layer = turn // 2, turn % 2
    half = turn % 2

    first = me_ref[0] * 2
    offs = [offset_ref[n % 8, first + n // 8] for n in range(ITEMS)]
    places = []
    for k in range(BOUNDS):
        own = offset_ref[layer * BOUNDS + k, first + slot]
        number = turn_item = slot * 8 + layer * BOUNDS + k
        place = jnp.int32(0)
        for n in range(ITEMS):
            ahead = (offs[n] > own) | ((offs[n] == own) & (n < turn_item))
            place = place + ahead.astype(jnp.int32)
        places.append(place)

    def wait(which, k):
        pltpu.make_async_copy(held.at[which, k], pieces[0].at[0], sems.at[which, k]).wait()

    before = conv_state_ref[0].astype(F32)
    ext[5:8, :] = jnp.where(slot == 0, before[:, 0, :], before[:, 1, :])
    ext[8:264, :] = conv_in_ref[0, 0].astype(F32)
    taps = taps_ref[0].astype(F32)
    shift = shift_ref[0]
    for c in range(6):
        cols = slice(128 * c, 128 * (c + 1))
        summed = shift[:, cols]
        for k in range(4):
            summed = summed + taps[k : k + 1, cols] * ext[5 + k : 261 + k, cols]
        active_ref[0, :, cols] = silu(summed).astype(BF16)

    rows = lax.broadcasted_iota(jnp.int32, (8, 256), 0)
    bias = jnp.zeros((8, 256), F32)
    rate = jnp.zeros((8, 256), F32)
    for h in range(8):
        bias = jnp.where(rows == h, bias_ref[layer, h], bias)
        rate = jnp.where(rows == h, decay_ref[layer, h], rate)
    raw = step_ref[0, 0].astype(F32) + bias
    soft = jnp.maximum(raw, 0.0) + jnp.log1p(jnp.exp(-jnp.abs(raw)))
    here = lax.broadcasted_iota(jnp.int32, (8, 256), 1) < length_ref[slot]
    size = jnp.where(here, soft, 0.0)
    drop = size * (-jnp.exp(rate))
    hi = drop.astype(BF16)
    rest = drop - hi.astype(F32)
    mid = rest.astype(BF16)
    low = (rest - mid.astype(F32)).astype(BF16)
    upto = (
        lax.broadcasted_iota(jnp.int32, (256, 256), 0)
        <= lax.broadcasted_iota(jnp.int32, (256, 256), 1)
    ).astype(F32).astype(BF16)
    cum = (
        jnp.dot(low, upto, preferred_element_type=F32)
        + jnp.dot(mid, upto, preferred_element_type=F32)
        + jnp.dot(hi, upto, preferred_element_type=F32)
    )
    cum_ref[0] = cum
    size_ref[0] = size

    lane = lax.broadcasted_iota(jnp.int32, (8, 256), 1)
    ends = [cum[:, 64 * k + 63 : 64 * k + 64] for k in range(BOUNDS)]
    last = ends[3]
    for k in (2, 1, 0):
        last = jnp.where(lane < 64 * (k + 1), ends[k], last)
    share = jnp.exp(last - cum) * size
    fade = [jnp.exp(ends[0])] + [jnp.exp(ends[k] - ends[k - 1]) for k in range(1, BOUNDS)]
    x_turned = active_ref[0, :, 0:512].astype(F32).T
    b_rows = active_ref[0, :, 512:640]
    row = lax.broadcasted_iota(jnp.int32, (128, 128), 0)
    pairs = []
    for p in range(2):
        b_here = b_rows[128 * p : 128 * (p + 1)]
        zero = jnp.zeros_like(b_here)
        pairs.append(
            jnp.concatenate(
                [jnp.where(row < 64, b_here, zero), jnp.where(row < 64, zero, b_here)], axis=1
            )
        )

    @pl.when(turn >= 2)
    def _():
        for k in range(BOUNDS):
            wait(half, k)

    for h in range(8):
        part = slice(64 * h, 64 * (h + 1))
        scaled = (x_turned[part] * share[h : h + 1]).astype(BF16)
        grown = [
            jnp.dot(scaled[:, 128 * p : 128 * (p + 1)], pairs[p], preferred_element_type=F32)
            for p in range(2)
        ]
        state = init_ref[0, 0, part, :].astype(F32)
        for k in range(BOUNDS):
            more = grown[k // 2][:, 128 * (k % 2) : 128 * (k % 2 + 1)]
            state = state * fade[k][h : h + 1] + more
            held[half, k, part, :] = state.astype(BF16)

    for k in range(BOUNDS):
        start = jnp.minimum(length_ref[slot], 64 * (k + 1)) + 5
        for r in range(3):
            line = ext[pl.ds(start + r, 1), :]
            for c in range(6):
                tail[r * 6 + c : r * 6 + c + 1, :] = line[:, 128 * c : 128 * (c + 1)]
        tail[18:32, :] = jnp.zeros((14, 128), F32)
        held[half, k, STATE_ROWS:ITEM_ROWS, :] = tail[...].astype(BF16)

    for k in range(BOUNDS):
        for n, piece in enumerate(pieces):

            @pl.when((places[k] >= CUTS[n]) & (places[k] < CUTS[n + 1]))
            def _():
                pltpu.make_async_copy(
                    held.at[half, k], piece.at[places[k] - CUTS[n]], sems.at[half, k]
                ).start()

    @pl.when(turn == 3)
    def _():
        for which in range(2):
            for k in range(BOUNDS):
                wait(which, k)


def make_states(me, offsets, lengths, step_bias, decay_log, conv_in, conv_state, taps, shift, step, init):
    return pl.pallas_call(
        states_kernel,
        grid_spec=pltpu.PrefetchScalarGridSpec(
            num_scalar_prefetch=5,
            grid=(4,),
            in_specs=[
                pl.BlockSpec((8, 64), lambda g, *_: (0, 0)),
                pl.BlockSpec((1, 1, 256, 768), lambda g, *_: (g % 2, g // 2, 0, 0)),
                pl.BlockSpec((1, 3, 2, 768), lambda g, *_: (g % 2, 0, 0, 0)),
                pl.BlockSpec((1, 4, 768), lambda g, *_: (g % 2, 0, 0)),
                pl.BlockSpec((1, 1, 768), lambda g, *_: (g % 2, 0, 0)),
                pl.BlockSpec((1, 1, 8, 256), lambda g, *_: (g % 2, g // 2, 0, 0)),
                pl.BlockSpec((1, 1, 512, 128), lambda g, *_: (g % 2, g // 2, 0, 0)),
            ],
            out_specs=[
                pl.BlockSpec((1, 256, 768), lambda g, *_: (g, 0, 0)),
                pl.BlockSpec((1, 8, 256), lambda g, *_: (g, 0, 0)),
                pl.BlockSpec((1, 8, 256), lambda g, *_: (g, 0, 0)),
                pl.BlockSpec(memory_space=pltpu.SMEM),
            ]
            + [pl.BlockSpec(memory_space=pl.ANY)] * len(SIZES),
            scratch_shapes=[
                pltpu.VMEM((264, 768), F32),
                pltpu.VMEM((TAIL_ROWS, 128), F32),
                pltpu.VMEM((2, BOUNDS, ITEM_ROWS, 128), BF16),
                pltpu.SemaphoreType.DMA((2, BOUNDS)),
            ],
        ),
        out_shape=[
            jax.ShapeDtypeStruct((4, 256, 768), BF16),
            jax.ShapeDtypeStruct((4, 8, 256), F32),
            jax.ShapeDtypeStruct((4, 8, 256), F32),
            jax.ShapeDtypeStruct((1,), jnp.int32),
        ]
        + [jax.ShapeDtypeStruct((rows, ITEM_ROWS, 128), BF16) for rows in SIZES],
        compiler_params=pltpu.CompilerParams(vmem_limit_bytes=VMEM_BYTES),
        cost_estimate=pl.CostEstimate(flops=10**9, bytes_accessed=8 * 2**20, transcendentals=10**6),
        name="states",
    )(me, offsets, lengths, step_bias, decay_log, offsets, conv_in, conv_state, taps, shift, step, init)


def mixed_kernel(
    me_ref,
    length_ref,
    skip_ref,
    active_ref,
    cum_ref,
    size_ref,
    init_ref,
    gate_ref,
    gain_ref,
    weight_ref,
    mine_ref,
    theirs_ref,
    gated,
    carried,
    scores,
    columns,
):
    layer, slot = pl.program_id(0) // 2, pl.program_id(0) % 2
    chip, core = me_ref[1] >> 1, me_ref[1] & 1
    b_rows = active_ref[0, :, 512:640]
    c_rows = active_ref[0, :, 640:768]
    nt = (((1,), (1,)), ((), ()))
    scores[...] = lax.dot_general(c_rows, b_rows, nt, preferred_element_type=F32)
    carried[...] = lax.dot_general(c_rows, init_ref[0, 0], nt, preferred_element_type=F32)
    turned = jnp.concatenate([cum_ref[0], jnp.zeros((120, 256), F32)], axis=0).T
    for h in range(8):
        columns[h] = turned[:, h : h + 1]
    low_lane = lax.broadcasted_iota(jnp.int32, (256, 128), 1) < 64
    causal = lax.broadcasted_iota(jnp.int32, (128, 128), 0) >= lax.broadcasted_iota(
        jnp.int32, (128, 128), 1
    )

    def pair(p, squares):
        cols = pl.ds(pl.multiple_of(128 * p, 128), 128)
        x_pair = active_ref[0, :, cols]
        halves = []
        for h in (2 * p, 2 * p + 1):
            row_cum = cum_ref[0, pl.ds(h, 1), :]
            row_size = size_ref[0, pl.ds(h, 1), :]
            col = columns[h]
            top = jnp.where(causal, jnp.exp(jnp.where(causal, col[:128] - row_cum[:, :128], 0.0)), 0.0)
            top = (scores[:128, :128] * top * row_size[:, :128]).astype(BF16)
            left = jnp.exp(col[128:] - row_cum[:, :128])
            left = (scores[128:, :128] * left * row_size[:, :128]).astype(BF16)
            right = jnp.where(causal, jnp.exp(jnp.where(causal, col[128:] - row_cum[:, 128:], 0.0)), 0.0)
            right = (scores[128:, 128:] * right * row_size[:, 128:]).astype(BF16)
            upper = jnp.dot(top, x_pair[:128], preferred_element_type=F32)
            lower = jnp.dot(
                jnp.concatenate([left, right], axis=1), x_pair, preferred_element_type=F32
            )
            halves.append(jnp.concatenate([upper, lower], axis=0))
        inner = jnp.where(low_lane, halves[0], halves[1])
        growth = jnp.exp(jnp.where(low_lane, columns[2 * p], columns[2 * p + 1]))
        skip = jnp.where(low_lane, skip_ref[layer, 2 * p], skip_ref[layer, 2 * p + 1])
        output = inner + carried[:, cols] * growth + skip * x_pair.astype(F32)
        product = output * silu(gate_ref[0, 0, :, cols].astype(F32))
        gated[:, cols] = product
        return squares + jnp.sum(product * product, axis=1, keepdims=True)

    squares = lax.fori_loop(0, 4, pair, jnp.zeros((256, 1), F32))
    inverse = lax.rsqrt(squares * (1.0 / 512.0) + EPS)
    valid = lax.broadcasted_iota(jnp.int32, (256, 1), 0) < length_ref[slot]
    normed = gated[...] * inverse * gain_ref[pl.ds(layer, 1), :]
    normed = jnp.where(valid, normed, 0.0).astype(BF16)

    def block(away, carry):
        for out_ref, its_core in ((mine_ref, core), (theirs_ref, 1 - core)):
            at = pl.multiple_of((((chip + away) & 3) * 2 + its_core) * 256, 256)
            out_ref[away] = jnp.dot(
                normed, weight_ref[0, :, pl.ds(at, 256)], preferred_element_type=F32
            ).astype(BF16)
        return carry

    lax.fori_loop(0, 4, block, 0)


def make_mixed(me, lengths, skip, active, cum, size, init, gate, gain, weight):
    return pl.pallas_call(
        mixed_kernel,
        grid_spec=pltpu.PrefetchScalarGridSpec(
            num_scalar_prefetch=3,
            grid=(4,),
            in_specs=[
                pl.BlockSpec((1, 256, 768), lambda g, *_: (2 * (g % 2) + g // 2, 0, 0)),
                pl.BlockSpec((1, 8, 256), lambda g, *_: (2 * (g % 2) + g // 2, 0, 0)),
                pl.BlockSpec((1, 8, 256), lambda g, *_: (2 * (g % 2) + g // 2, 0, 0)),
                pl.BlockSpec((1, 1, 512, 128), lambda g, *_: (g // 2, g % 2, 0, 0)),
                pl.BlockSpec((1, 1, 256, 512), lambda g, *_: (g // 2, g % 2, 0, 0)),
                pl.BlockSpec((2, 512), lambda g, *_: (0, 0)),
                pl.BlockSpec((1, 512, 2048), lambda g, *_: (g // 2, 0, 0)),
            ],
            out_specs=[pl.BlockSpec((4, 256, 256), lambda g, *_: (0, g, 0))] * 2,
            scratch_shapes=[
                pltpu.VMEM((256, 512), F32),
                pltpu.VMEM((256, 512), F32),
                pltpu.VMEM((256, 256), F32),
                pltpu.VMEM((8, 256, 1), F32),
            ],
        ),
        out_shape=[jax.ShapeDtypeStruct((4, 1024, 256), BF16)] * 2,
        compiler_params=pltpu.CompilerParams(vmem_limit_bytes=VMEM_BYTES),
        cost_estimate=pl.CostEstimate(flops=10**7, bytes_accessed=2**20, transcendentals=0),
        name="mixed",
    )(me, lengths, skip, active, cum, size, init, gate, gain, weight)


def total_kernel(*refs):
    total = refs[0][...].astype(F32)
    for part in refs[1:4]:
        total = total + part[...].astype(F32)
    refs[4][...] = total.astype(BF16)


def make_total(parts):
    return pl.pallas_call(
        total_kernel,
        out_shape=jax.ShapeDtypeStruct((1024, 256), BF16),
        compiler_params=pltpu.CompilerParams(vmem_limit_bytes=VMEM_BYTES),
        name="total",
    )(*parts)


def to_device(array, pairs):
    return lax.ppermute(array, "tp", pairs)


def plan_kernel(me_ref, hit_off_ref, hit_row_ref, store_ref, *refs):
    base_refs, plan_ref = refs[:WINDOW], refs[WINDOW]
    me = me_ref[0]
    count = 512
    offs = store_ref[...]
    item = lax.broadcasted_iota(jnp.int32, (1, count), 1)
    source = item >> 4
    owner = (source + offs) & 31
    nearby = (owner + 32 - me) & 31
    base = jnp.zeros((1, count), jnp.int32)
    for n in range(WINDOW):
        base = jnp.where(nearby == n, base_refs[n][0], base)
    row = lax.broadcasted_iota(jnp.int32, (count, count), 0)
    col = lax.broadcasted_iota(jnp.int32, (count, count), 1)
    before = row < col
    together = (row >> 4) == (col >> 4)

    def ones(mask):
        return jnp.where(mask, 1.0, 0.0).astype(BF16)

    owned = lax.broadcasted_iota(jnp.int32, (32, count), 0) == owner
    ranks = jnp.dot(ones(owned), ones(before), preferred_element_type=F32)
    rank = jnp.sum(jnp.where(owned, ranks, 0.0), axis=0, keepdims=True).astype(jnp.int32)
    distance = lax.broadcasted_iota(jnp.int32, (16, count), 0)
    alike = ones(distance == offs)
    inside = jnp.dot(alike, ones(before & together), preferred_element_type=F32)
    total = jnp.dot(alike, ones(together), preferred_element_type=F32)
    place = jnp.sum(
        jnp.where(distance == offs, inside, 0.0) + jnp.where(distance > offs, total, 0.0),
        axis=0,
        keepdims=True,
    ).astype(jnp.int32)
    target = (base + rank) & 15
    code = (1 + offs * 16 + place).astype(F32)
    key = jnp.where((rank < 16) & (nearby < WINDOW), owner * 16 + target, -1)
    number = lax.broadcasted_iota(jnp.int32, (32, count), 0)
    wanted = me * 16 + number
    for b in range(WINDOW):
        asker = (me + 32 - b) & 31
        for j in range(4):
            slot = asker * 2 + j // 2
            place_wanted = ((asker + hit_off_ref[j % 2, slot]) & 31) * 16 + hit_row_ref[j % 2, slot]
            wanted = jnp.where(number == 16 + 4 * b + j, place_wanted, wanted)
    found = jnp.sum(jnp.where(wanted == key, code, 0.0), axis=1, keepdims=True)
    plan_ref[...] = jnp.broadcast_to(found, (32, 128)).astype(jnp.int32)


def make_plan(me, hit_off, hit_row, store_row, bases):
    smem = pl.BlockSpec(memory_space=pltpu.SMEM)
    return pl.pallas_call(
        plan_kernel,
        in_specs=[smem, smem, smem, pl.BlockSpec(memory_space=pltpu.VMEM)] + [smem] * WINDOW,
        out_specs=pl.BlockSpec(memory_space=pltpu.VMEM),
        out_shape=jax.ShapeDtypeStruct((32, 128), jnp.int32),
        compiler_params=pltpu.CompilerParams(vmem_limit_bytes=VMEM_BYTES),
        name="plan",
    )(me, hit_off, hit_row, store_row, *bases)


def asked(plan_ref, hit_off_ref, hit_row_ref, me, back):
    asker = (me + 32 - back) & 31
    deltas, numbers, places, rows, founds = [], [], [], [], []
    for j in range(4):
        slot = asker * 2 + j // 2
        off = hit_off_ref[j % 2, slot]
        code = plan_ref[16 + 4 * back + j, 0]
        found = code > 0
        delta = off - jnp.where(found, (code - 1) >> 4, 0)
        number = jnp.int32(0)
        for other in deltas:
            number = number + (other == delta).astype(jnp.int32)
        deltas.append(delta)
        numbers.append(number)
        places.append((code - 1) & 15)
        rows.append(hit_row_ref[j % 2, slot])
        founds.append(found)
    return deltas, numbers, places, rows, founds


def start_from(pieces, place, start):
    for piece, begin, end in pieces:

        @pl.when((place >= begin) & (place < end))
        def _():
            start(piece, place - begin)


def serve_kernel(me_ref, plan_ref, hit_off_ref, hit_row_ref, *refs):
    pieces = [(refs[n], CUTS[n], CUTS[n + 1]) for n in range(len(SIZES))]
    pool_ref, pool_conv_ref, far_ref, near_ref = refs[len(SIZES) : len(SIZES) + 4]
    lines, tail, packed, jobs, sems, tail_sems = refs[len(SIZES) + 4 :]
    lines[...] = pool_conv_ref[...].astype(F32)
    tail[18:32, :] = jnp.zeros((14, 128), F32)
    for d in range(1, WINDOW):
        deltas, numbers, places, rows, founds = asked(
            plan_ref, hit_off_ref, hit_row_ref, me_ref[0], d
        )
        for j in range(4):
            wanted = (deltas[j] == d) & (numbers[j] < DOWN[d - 1])
            jobs[0, 4 * d + j] = jnp.where(wanted, jnp.where(founds[j], 1, 2), 0)
            jobs[1, 4 * d + j] = jnp.minimum(numbers[j], DOWN[d - 1] - 1)
            jobs[2, 4 * d + j] = jnp.where(founds[j], places[j], rows[j])

    for d in range(1, WINDOW):
        out, begin = ((near_ref, 0), (far_ref, DOWN[2]), (far_ref, 0))[d - 1]

        def dest(n):
            return out.at[begin + jobs[1, n]]

        def state(n):
            return pltpu.make_async_copy(
                pool_ref.at[jobs[2, n]], dest(n).at[pl.ds(0, STATE_ROWS)], sems.at[n]
            )

        def rest(n):
            return pltpu.make_async_copy(
                packed.at[n], dest(n).at[pl.ds(STATE_ROWS, TAIL_ROWS)], tail_sems.at[n]
            )

        def begin_job(j, carry):
            n = 4 * d + j

            @pl.when(jobs[0, n] == 1)
            def _():
                start_from(
                    pieces,
                    jobs[2, n],
                    lambda piece, row: pltpu.make_async_copy(
                        piece.at[row], dest(n), sems.at[n]
                    ).start(),
                )

            @pl.when(jobs[0, n] == 2)
            def _():
                state(n).start()
                for r in range(3):
                    line = lines[r, pl.ds(jobs[2, n], 1), :]
                    for c in range(6):
                        tail[r * 6 + c : r * 6 + c + 1, :] = line[:, 128 * c : 128 * (c + 1)]
                packed[n] = tail[...].astype(BF16)
                rest(n).start()

            return carry

        def end_job(j, carry):
            n = 4 * d + j

            @pl.when(jobs[0, n] == 1)
            def _():
                pltpu.make_async_copy(pieces[0][0].at[0], dest(n), sems.at[n]).wait()

            @pl.when(jobs[0, n] == 2)
            def _():
                state(n).wait()
                rest(n).wait()

            return carry

        lax.fori_loop(0, 4, begin_job, 0)
        lax.fori_loop(0, 4, end_job, 0)


def serve(me, plan, hit_off, hit_row, pieces, pool, pool_conv):
    smem = pl.BlockSpec(memory_space=pltpu.SMEM)
    hbm = pl.BlockSpec(memory_space=pl.ANY)
    vmem = pl.BlockSpec(memory_space=pltpu.VMEM)
    return pl.pallas_call(
        serve_kernel,
        in_specs=[smem] * 4 + [hbm] * (len(SIZES) + 1) + [vmem],
        out_specs=[vmem] * 2,
        out_shape=[
            jax.ShapeDtypeStruct((DOWN[1] + DOWN[2], ITEM_ROWS, 128), BF16),
            jax.ShapeDtypeStruct((DOWN[0], ITEM_ROWS, 128), BF16),
        ],
        scratch_shapes=[
            pltpu.VMEM((3, 16, 768), F32),
            pltpu.VMEM((TAIL_ROWS, 128), F32),
            pltpu.VMEM((16, TAIL_ROWS, 128), BF16),
            pltpu.SMEM((3, 16), jnp.int32),
            pltpu.SemaphoreType.DMA((16,)),
            pltpu.SemaphoreType.DMA((16,)),
        ],
        compiler_params=pltpu.CompilerParams(vmem_limit_bytes=VMEM_BYTES),
        name="serve",
    )(me, plan, hit_off, hit_row, *pieces, pool, pool_conv)


def settle_kernel(layout, me_ref, plan_ref, hit_off_ref, hit_row_ref, *refs):
    count = len(layout)
    by_hop = [
        [(refs[n], CUTS[piece], CUTS[piece + 1]) for n, (at, piece) in enumerate(layout) if at == hop]
        for hop in range(WINDOW)
    ]
    two_ref, last_ref, pool_ref, pool_conv_ref = refs[count : count + 4]
    pool_out, pool_conv_out, next_out, next_conv_out = refs[count + 4 : count + 8]
    lines, next_lines, tails, wide, sems, tail_sems = refs[count + 8 :]

    def state_of(source, dest, n):
        return pltpu.make_async_copy(source, dest, sems.at[n])

    def tail_of(source, n):
        return pltpu.make_async_copy(source, tails.at[n], tail_sems.at[n])

    def start_item(array, index, dest, n):
        state_of(array.at[index, pl.ds(0, STATE_ROWS)], dest, n).start()
        tail_of(array.at[index, pl.ds(STATE_ROWS, TAIL_ROWS)], n).start()

    def from_items(hop, place, dest, n):
        for at, pieces in enumerate(by_hop):

            @pl.when(hop == at)
            def _():
                start_from(pieces, place, lambda piece, row: start_item(piece, row, dest, n))

    def begin_row(n, carry):
        code = plan_ref[n, 0]

        @pl.when(code == 0)
        def _():
            state_of(pool_ref.at[n], pool_out.at[n], n).start()

        @pl.when(code > 0)
        def _():
            from_items((code - 1) >> 4, (code - 1) & 15, pool_out.at[n], n)

        return carry

    lax.fori_loop(0, ITEMS, begin_row, 0)

    deltas, numbers, places, rows, founds = asked(
        plan_ref, hit_off_ref, hit_row_ref, me_ref[0], 0
    )
    kept = []
    for j in range(4):
        n = ITEMS + j
        dest = next_out.at[j % 2, j // 2]
        here = jnp.logical_not(founds[j]) & (deltas[j] == 0)
        kept.append(here)

        @pl.when(here)
        def _():
            state_of(pool_ref.at[rows[j]], dest, n).start()

        @pl.when(founds[j] & (deltas[j] <= 0))
        def _():
            from_items(-deltas[j], places[j], dest, n)

        for d in range(1, WINDOW):
            array, begin = ((last_ref, DOWN[2]), (two_ref, DOWN[2]), (last_ref, 0))[d - 1]

            @pl.when(deltas[j] == d)
            def _():
                start_item(array, begin + jnp.minimum(numbers[j], DOWN[d - 1] - 1), dest, n)

    lines[...] = pool_conv_ref[...].astype(F32)
    some_tail = last_ref.at[0, pl.ds(STATE_ROWS, TAIL_ROWS)]

    for j in range(4):
        n = ITEMS + j

        @pl.when(kept[j])
        def _():
            for r in range(3):
                next_lines[j % 2, r, j // 2 : j // 2 + 1, :] = lines[r, pl.ds(rows[j], 1), :]

        @pl.when(jnp.logical_not(kept[j]))
        def _():
            tail_of(some_tail, n).wait()
            tail = tails[n].astype(F32)
            for r in range(3):
                for c in range(6):
                    next_lines[j % 2, r, j // 2 : j // 2 + 1, 128 * c : 128 * (c + 1)] = tail[
                        r * 6 + c : r * 6 + c + 1
                    ]

    def end_tail(n, carry):
        @pl.when(plan_ref[n, 0] > 0)
        def _():
            tail_of(some_tail, n).wait()

        return carry

    lax.fori_loop(0, ITEMS, end_tail, 0)
    wide[...] = tails[0:ITEMS].astype(F32)
    stored = jnp.zeros((ITEMS, 128), jnp.int32)
    row = lax.broadcasted_iota(jnp.int32, (ITEMS, 128), 0)
    for n in range(ITEMS):
        stored = jnp.where(row == n, plan_ref[n, 0], stored)
    for r in range(3):
        for c in range(6):
            cols = slice(128 * c, 128 * (c + 1))
            lines[r, :, cols] = jnp.where(stored > 0, wide[:, r * 6 + c, :], lines[r, :, cols])

    def end_row(n, carry):
        state_of(pool_ref.at[0], pool_out.at[n], n).wait()
        return carry

    lax.fori_loop(0, ITEMS, end_row, 0)
    pool_conv_out[...] = lines[...].astype(BF16)
    next_conv_out[...] = next_lines[...].astype(BF16)
    for j in range(4):
        state_of(pool_ref.at[0], next_out.at[j % 2, j // 2], ITEMS + j).wait()


def settle(layout, me, plan, hit_off, hit_row, received, two, last, pool, pool_conv):
    smem = pl.BlockSpec(memory_space=pltpu.SMEM)
    hbm = pl.BlockSpec(memory_space=pl.ANY)
    vmem = pl.BlockSpec(memory_space=pltpu.VMEM)
    return pl.pallas_call(
        functools.partial(settle_kernel, layout),
        in_specs=[smem] * 4 + [hbm] * (len(layout) + 3) + [vmem],
        out_specs=[vmem] * 4,
        out_shape=[
            jax.ShapeDtypeStruct((16, STATE_ROWS, 128), BF16),
            jax.ShapeDtypeStruct((3, 16, 768), BF16),
            jax.ShapeDtypeStruct((2, 2, STATE_ROWS, 128), BF16),
            jax.ShapeDtypeStruct((2, 3, 2, 768), BF16),
        ],
        scratch_shapes=[
            pltpu.VMEM((3, 16, 768), F32),
            pltpu.VMEM((2, 3, 2, 768), F32),
            pltpu.VMEM((ITEMS + 4, TAIL_ROWS, 128), BF16),
            pltpu.VMEM((ITEMS, TAIL_ROWS, 128), F32),
            pltpu.SemaphoreType.DMA((ITEMS + 4,)),
            pltpu.SemaphoreType.DMA((ITEMS + 4,)),
        ],
        compiler_params=pltpu.CompilerParams(vmem_limit_bytes=VMEM_BYTES),
        name="settle",
    )(me, plan, hit_off, hit_row, *received, two, last, pool, pool_conv)


def after(value, *others):
    return lax.optimization_barrier((value,) + others)[0]


def body(
    conv_input,
    conv_weight,
    conv_bias,
    step_raw,
    step_bias,
    decay_log,
    skip_weight,
    gate_input,
    norm_gain,
    out_weight,
    ssm_state,
    conv_state,
    pool_ssm,
    pool_conv,
    lengths,
    store_offset,
    store_base,
    hit_offset,
    hit_row,
):
    me = jnp.stack([lax.axis_index("cache"), lax.axis_index("tp")]).astype(jnp.int32)
    offsets = jnp.transpose(store_offset, (1, 2, 0)).reshape(8, 64)
    hit_off = jnp.transpose(hit_offset, (1, 2, 0)).reshape(2, 64)
    hit_at = hit_row.T
    init = ssm_state.reshape(2, 2, STATE_ROWS, 128)
    pool = pool_ssm.reshape(16, STATE_ROWS, 128)
    pool_lines = jnp.transpose(pool_conv, (1, 2, 0, 3)).reshape(3, 16, 768)
    conv_lines = jnp.transpose(conv_state, (0, 2, 3, 1, 4)).reshape(2, 3, 2, 768)

    active, cum, size, more, *pieces = make_states(
        me,
        offsets,
        lengths,
        step_bias,
        decay_log,
        conv_input.reshape(2, 2, 256, 768),
        conv_lines,
        conv_weight.reshape(2, 4, 768),
        conv_bias,
        step_raw,
        init,
    )
    first = [passed_along(piece, 1) for piece in pieces[:3]]
    base = after(store_base, *pieces)
    bases = [base if n == 0 else passed_along(base, -n) for n in range(WINDOW)]
    plan = make_plan(me, hit_off, hit_at, store_offset.reshape(1, 512), bases)
    served, near = serve(me, plan, hit_off, hit_at, pieces, pool, pool_lines)
    one = passed_along(served, -1)
    mine, theirs = make_mixed(
        me,
        lengths,
        skip_weight,
        after(active, served),
        cum,
        size,
        init,
        gate_input,
        norm_gain,
        out_weight,
    )
    first, one, near, mine, theirs = lax.optimization_barrier((first, one, near, mine, theirs))

    second = [passed_along(first[n], 1) for n in range(2)]
    two = passed_along(one, -1)
    other = lax.ppermute(theirs, "tp", [(i, i ^ 1) for i in range(8)])
    sums = [(mine[away].astype(F32) + other[away].astype(F32)).astype(BF16) for away in range(4)]
    mixed = make_total(
        [sums[0]]
        + [
            lax.ppermute(sums[away], "tp", [(i, (i + 2 * away) % 8) for i in range(8)])
            for away in (1, 2, 3)
        ]
    )

    def follow(parts):
        late = passed_along(parts[0], 1)
        return [late, passed_along(late, 1), passed_along(parts[1], 1)]

    extra = lax.cond(
        more[0] > 0,
        follow,
        lambda parts: [parts[0], parts[0], parts[1]],
        [pieces[3], first[2]],
    )
    second, two, near, mixed, extra = lax.optimization_barrier((second, two, near, mixed, extra))

    third = passed_along(second[0], 1)
    last = passed_along(jnp.concatenate([two[: DOWN[2]], near]), -1)
    layout = ((0, 0), (0, 1), (0, 2), (0, 3), (1, 0), (1, 1), (1, 2), (2, 0), (2, 1), (3, 0))
    layout += ((1, 3), (2, 3), (2, 2))
    pool_out, pool_lines_out, next_ssm, next_lines = settle(
        layout,
        me,
        plan,
        hit_off,
        hit_at,
        [*pieces, *first, *second, third, *extra],
        two,
        last,
        pool,
        pool_lines,
    )
    return (
        mixed.reshape(2, 2, 256, 256),
        pool_out.reshape(pool_ssm.shape),
        jnp.transpose(pool_lines_out.reshape(3, 1, 16, 768), (2, 0, 1, 3)),
        next_ssm.reshape(ssm_state.shape),
        jnp.transpose(next_lines.reshape(2, 3, 1, 2, 768), (0, 3, 1, 2, 4)),
    )


def solution(mesh):
    in_specs = (
        P(None, "cache", None, "tp", None),
        P(None, None, "tp", None),
        P(None, "tp", None),
        P(None, "cache", "tp", None),
        P(None, "tp"),
        P(None, "tp"),
        P(None, "tp"),
        P(None, "cache", None, "tp"),
        P(None, "tp"),
        P(None, "tp", None),
        P(None, "cache", "tp", None, None),
        P(None, "cache", None, "tp", None),
        P("cache", "tp", None, None),
        P("cache", None, "tp", None),
        P("cache"),
        P(),
        P("cache"),
        P(),
        P(),
    )
    out_specs = (
        P(None, "cache", None, "tp"),
        P("cache", "tp", None, None),
        P("cache", None, "tp", None),
        P(None, "cache", "tp", None, None),
        P(None, "cache", None, "tp", None),
    )
    return jax.shard_map(body, mesh=mesh, in_specs=in_specs, out_specs=out_specs, check_vma=False)
```

```python
import functools

import jax
import jax.numpy as jnp
from jax import lax
from jax.experimental import pallas as pl
from jax.experimental.pallas import tpu as pltpu
from jax.sharding import PartitionSpec as P

BOUNDS = 4
WINDOW = 4
EPS = 1e-05
STATE_ROWS = 512
ITEM_ROWS = 544
TAIL_ROWS = 32
ITEMS = 16
VMEM_BYTES = 60 * 2**20
F32 = jnp.float32
BF16 = jnp.bfloat16
CUTS = (0, 8, 12, 14, 16)
SIZES = tuple(end - begin for begin, end in zip(CUTS, CUTS[1:]))
THIRD = (5, 8)
DOWN = (4, 4, 2)


def passed_along(array, by):
    size = lax.axis_size("cache")
    return lax.ppermute(array, "cache", [(i, (i + by) % size) for i in range(size)])


def silu(v):
    return 0.5 * v * (1.0 + jnp.tanh(0.5 * v))


def states_kernel(
    me_ref,
    offset_ref,
    length_ref,
    bias_ref,
    decay_ref,
    offsets_ref,
    conv_in_ref,
    conv_state_ref,
    taps_ref,
    shift_ref,
    step_ref,
    init_ref,
    active_ref,
    cum_ref,
    size_ref,
    more_ref,
    *refs,
):
    pieces = refs[: len(SIZES)]
    ext, tail, held, sems = refs[len(SIZES) :]
    turn = pl.program_id(0)

    @pl.when(turn == 0)
    def _():
        offsets = offsets_ref[...]
        even = lax.broadcasted_iota(jnp.int32, (1, 64), 1) % 2 == 0
        far = []
        for n in range(1, WINDOW):
            of_slot = jnp.sum(jnp.where(offsets >= n, 1.0, 0.0), axis=0, keepdims=True)
            after_it = jnp.concatenate([of_slot[:, 1:], of_slot[:, :1]], axis=1)
            far.append(jnp.max(jnp.where(even, of_slot + after_it, 0.0)).astype(jnp.int32))
        more_ref[0] = ((far[0] > CUTS[3]) | (far[1] > CUTS[2])).astype(jnp.int32)
        more_ref[1] = (far[1] > CUTS[1]).astype(jnp.int32)
        more_ref[2] = (far[2] > THIRD[0]).astype(jnp.int32)

    slot, layer = turn // 2, turn % 2
    half = turn % 2

    first = me_ref[0] * 2
    offs = [offset_ref[n % 8, first + n // 8] for n in range(ITEMS)]
    places = []
    for k in range(BOUNDS):
        own = offset_ref[layer * BOUNDS + k, first + slot]
        number = turn_item = slot * 8 + layer * BOUNDS + k
        place = jnp.int32(0)
        for n in range(ITEMS):
            ahead = (offs[n] > own) | ((offs[n] == own) & (n < turn_item))
            place = place + ahead.astype(jnp.int32)
        places.append(place)

    def wait(which, k):
        pltpu.make_async_copy(held.at[which, k], pieces[0].at[0], sems.at[which, k]).wait()

    before = conv_state_ref[0].astype(F32)
    ext[5:8, :] = jnp.where(slot == 0, before[:, 0, :], before[:, 1, :])
    ext[8:264, :] = conv_in_ref[0, 0].astype(F32)
    taps = taps_ref[0].astype(F32)
    shift = shift_ref[0]
    for c in range(6):
        cols = slice(128 * c, 128 * (c + 1))
        summed = shift[:, cols]
        for k in range(4):
            summed = summed + taps[k : k + 1, cols] * ext[5 + k : 261 + k, cols]
        active_ref[0, :, cols] = silu(summed).astype(BF16)

    rows = lax.broadcasted_iota(jnp.int32, (8, 256), 0)
    bias = jnp.zeros((8, 256), F32)
    rate = jnp.zeros((8, 256), F32)
    for h in range(8):
        bias = jnp.where(rows == h, bias_ref[layer, h], bias)
        rate = jnp.where(rows == h, decay_ref[layer, h], rate)
    raw = step_ref[0, 0].astype(F32) + bias
    soft = jnp.maximum(raw, 0.0) + jnp.log1p(jnp.exp(-jnp.abs(raw)))
    here = lax.broadcasted_iota(jnp.int32, (8, 256), 1) < length_ref[slot]
    size = jnp.where(here, soft, 0.0)
    drop = size * (-jnp.exp(rate))
    hi = drop.astype(BF16)
    rest = drop - hi.astype(F32)
    mid = rest.astype(BF16)
    low = (rest - mid.astype(F32)).astype(BF16)
    upto = (
        lax.broadcasted_iota(jnp.int32, (256, 256), 0)
        <= lax.broadcasted_iota(jnp.int32, (256, 256), 1)
    ).astype(F32).astype(BF16)
    cum = (
        jnp.dot(low, upto, preferred_element_type=F32)
        + jnp.dot(mid, upto, preferred_element_type=F32)
        + jnp.dot(hi, upto, preferred_element_type=F32)
    )
    cum_ref[0] = cum
    size_ref[0] = size

    lane = lax.broadcasted_iota(jnp.int32, (8, 256), 1)
    ends = [cum[:, 64 * k + 63 : 64 * k + 64] for k in range(BOUNDS)]
    last = ends[3]
    for k in (2, 1, 0):
        last = jnp.where(lane < 64 * (k + 1), ends[k], last)
    share = jnp.exp(last - cum) * size
    fade = [jnp.exp(ends[0])] + [jnp.exp(ends[k] - ends[k - 1]) for k in range(1, BOUNDS)]
    x_turned = active_ref[0, :, 0:512].astype(F32).T
    b_rows = active_ref[0, :, 512:640]
    row = lax.broadcasted_iota(jnp.int32, (128, 128), 0)
    pairs = []
    for p in range(2):
        b_here = b_rows[128 * p : 128 * (p + 1)]
        zero = jnp.zeros_like(b_here)
        pairs.append(
            jnp.concatenate(
                [jnp.where(row < 64, b_here, zero), jnp.where(row < 64, zero, b_here)], axis=1
            )
        )

    @pl.when(turn >= 2)
    def _():
        for k in range(BOUNDS):
            wait(half, k)

    for h in range(8):
        part = slice(64 * h, 64 * (h + 1))
        scaled = (x_turned[part] * share[h : h + 1]).astype(BF16)
        grown = [
            jnp.dot(scaled[:, 128 * p : 128 * (p + 1)], pairs[p], preferred_element_type=F32)
            for p in range(2)
        ]
        state = init_ref[0, 0, part, :].astype(F32)
        for k in range(BOUNDS):
            more = grown[k // 2][:, 128 * (k % 2) : 128 * (k % 2 + 1)]
            state = state * fade[k][h : h + 1] + more
            held[half, k, part, :] = state.astype(BF16)

    for k in range(BOUNDS):
        start = jnp.minimum(length_ref[slot], 64 * (k + 1)) + 5
        for r in range(3):
            line = ext[pl.ds(start + r, 1), :]
            for c in range(6):
                tail[r * 6 + c : r * 6 + c + 1, :] = line[:, 128 * c : 128 * (c + 1)]
        tail[18:32, :] = jnp.zeros((14, 128), F32)
        held[half, k, STATE_ROWS:ITEM_ROWS, :] = tail[...].astype(BF16)

    for k in range(BOUNDS):
        for n, piece in enumerate(pieces):

            @pl.when((places[k] >= CUTS[n]) & (places[k] < CUTS[n + 1]))
            def _():
                pltpu.make_async_copy(
                    held.at[half, k], piece.at[places[k] - CUTS[n]], sems.at[half, k]
                ).start()

    @pl.when(turn == 3)
    def _():
        for which in range(2):
            for k in range(BOUNDS):
                wait(which, k)


def make_states(me, offsets, lengths, step_bias, decay_log, conv_in, conv_state, taps, shift, step, init):
    return pl.pallas_call(
        states_kernel,
        grid_spec=pltpu.PrefetchScalarGridSpec(
            num_scalar_prefetch=5,
            grid=(4,),
            in_specs=[
                pl.BlockSpec((8, 64), lambda g, *_: (0, 0)),
                pl.BlockSpec((1, 1, 256, 768), lambda g, *_: (g % 2, g // 2, 0, 0)),
                pl.BlockSpec((1, 3, 2, 768), lambda g, *_: (g % 2, 0, 0, 0)),
                pl.BlockSpec((1, 4, 768), lambda g, *_: (g % 2, 0, 0)),
                pl.BlockSpec((1, 1, 768), lambda g, *_: (g % 2, 0, 0)),
                pl.BlockSpec((1, 1, 8, 256), lambda g, *_: (g % 2, g // 2, 0, 0)),
                pl.BlockSpec((1, 1, 512, 128), lambda g, *_: (g % 2, g // 2, 0, 0)),
            ],
            out_specs=[
                pl.BlockSpec((1, 256, 768), lambda g, *_: (g, 0, 0)),
                pl.BlockSpec((1, 8, 256), lambda g, *_: (g, 0, 0)),
                pl.BlockSpec((1, 8, 256), lambda g, *_: (g, 0, 0)),
                pl.BlockSpec(memory_space=pltpu.SMEM),
            ]
            + [pl.BlockSpec(memory_space=pl.ANY)] * len(SIZES),
            scratch_shapes=[
                pltpu.VMEM((264, 768), F32),
                pltpu.VMEM((TAIL_ROWS, 128), F32),
                pltpu.VMEM((2, BOUNDS, ITEM_ROWS, 128), BF16),
                pltpu.SemaphoreType.DMA((2, BOUNDS)),
            ],
        ),
        out_shape=[
            jax.ShapeDtypeStruct((4, 256, 768), BF16),
            jax.ShapeDtypeStruct((4, 8, 256), F32),
            jax.ShapeDtypeStruct((4, 8, 256), F32),
            jax.ShapeDtypeStruct((3,), jnp.int32),
        ]
        + [jax.ShapeDtypeStruct((rows, ITEM_ROWS, 128), BF16) for rows in SIZES],
        compiler_params=pltpu.CompilerParams(vmem_limit_bytes=VMEM_BYTES),
        cost_estimate=pl.CostEstimate(flops=10**9, bytes_accessed=8 * 2**20, transcendentals=10**6),
        name="states",
    )(me, offsets, lengths, step_bias, decay_log, offsets, conv_in, conv_state, taps, shift, step, init)


def mixed_kernel(
    me_ref,
    length_ref,
    skip_ref,
    active_ref,
    cum_ref,
    size_ref,
    init_ref,
    gate_ref,
    gain_ref,
    weight_ref,
    mine_ref,
    theirs_ref,
    gated,
    carried,
    scores,
    columns,
):
    layer, slot = pl.program_id(0) // 2, pl.program_id(0) % 2
    chip, core = me_ref[1] >> 1, me_ref[1] & 1
    b_rows = active_ref[0, :, 512:640]
    c_rows = active_ref[0, :, 640:768]
    nt = (((1,), (1,)), ((), ()))
    scores[...] = lax.dot_general(c_rows, b_rows, nt, preferred_element_type=F32)
    carried[...] = lax.dot_general(c_rows, init_ref[0, 0], nt, preferred_element_type=F32)
    turned = jnp.concatenate([cum_ref[0], jnp.zeros((120, 256), F32)], axis=0).T
    for h in range(8):
        columns[h] = turned[:, h : h + 1]
    low_lane = lax.broadcasted_iota(jnp.int32, (256, 128), 1) < 64
    causal = lax.broadcasted_iota(jnp.int32, (128, 128), 0) >= lax.broadcasted_iota(
        jnp.int32, (128, 128), 1
    )

    def pair(p, squares):
        cols = pl.ds(pl.multiple_of(128 * p, 128), 128)
        x_pair = active_ref[0, :, cols]
        halves = []
        for h in (2 * p, 2 * p + 1):
            row_cum = cum_ref[0, pl.ds(h, 1), :]
            row_size = size_ref[0, pl.ds(h, 1), :]
            col = columns[h]
            top = jnp.where(causal, jnp.exp(jnp.where(causal, col[:128] - row_cum[:, :128], 0.0)), 0.0)
            top = (scores[:128, :128] * top * row_size[:, :128]).astype(BF16)
            left = jnp.exp(col[128:] - row_cum[:, :128])
            left = (scores[128:, :128] * left * row_size[:, :128]).astype(BF16)
            right = jnp.where(causal, jnp.exp(jnp.where(causal, col[128:] - row_cum[:, 128:], 0.0)), 0.0)
            right = (scores[128:, 128:] * right * row_size[:, 128:]).astype(BF16)
            upper = jnp.dot(top, x_pair[:128], preferred_element_type=F32)
            lower = jnp.dot(
                jnp.concatenate([left, right], axis=1), x_pair, preferred_element_type=F32
            )
            halves.append(jnp.concatenate([upper, lower], axis=0))
        inner = jnp.where(low_lane, halves[0], halves[1])
        growth = jnp.exp(jnp.where(low_lane, columns[2 * p], columns[2 * p + 1]))
        skip = jnp.where(low_lane, skip_ref[layer, 2 * p], skip_ref[layer, 2 * p + 1])
        output = inner + carried[:, cols] * growth + skip * x_pair.astype(F32)
        product = output * silu(gate_ref[0, 0, :, cols].astype(F32))
        gated[:, cols] = product
        return squares + jnp.sum(product * product, axis=1, keepdims=True)

    squares = lax.fori_loop(0, 4, pair, jnp.zeros((256, 1), F32))
    inverse = lax.rsqrt(squares * (1.0 / 512.0) + EPS)
    valid = lax.broadcasted_iota(jnp.int32, (256, 1), 0) < length_ref[slot]
    normed = gated[...] * inverse * gain_ref[pl.ds(layer, 1), :]
    normed = jnp.where(valid, normed, 0.0).astype(BF16)

    def block(away, carry):
        for out_ref, its_core in ((mine_ref, core), (theirs_ref, 1 - core)):
            at = pl.multiple_of((((chip + away) & 3) * 2 + its_core) * 256, 256)
            out_ref[away] = jnp.dot(
                normed, weight_ref[0, :, pl.ds(at, 256)], preferred_element_type=F32
            ).astype(BF16)
        return carry

    lax.fori_loop(0, 4, block, 0)


def make_mixed(me, lengths, skip, active, cum, size, init, gate, gain, weight):
    return pl.pallas_call(
        mixed_kernel,
        grid_spec=pltpu.PrefetchScalarGridSpec(
            num_scalar_prefetch=3,
            grid=(4,),
            in_specs=[
                pl.BlockSpec((1, 256, 768), lambda g, *_: (2 * (g % 2) + g // 2, 0, 0)),
                pl.BlockSpec((1, 8, 256), lambda g, *_: (2 * (g % 2) + g // 2, 0, 0)),
                pl.BlockSpec((1, 8, 256), lambda g, *_: (2 * (g % 2) + g // 2, 0, 0)),
                pl.BlockSpec((1, 1, 512, 128), lambda g, *_: (g // 2, g % 2, 0, 0)),
                pl.BlockSpec((1, 1, 256, 512), lambda g, *_: (g // 2, g % 2, 0, 0)),
                pl.BlockSpec((2, 512), lambda g, *_: (0, 0)),
                pl.BlockSpec((1, 512, 2048), lambda g, *_: (g // 2, 0, 0)),
            ],
            out_specs=[pl.BlockSpec((4, 256, 256), lambda g, *_: (0, g, 0))] * 2,
            scratch_shapes=[
                pltpu.VMEM((256, 512), F32),
                pltpu.VMEM((256, 512), F32),
                pltpu.VMEM((256, 256), F32),
                pltpu.VMEM((8, 256, 1), F32),
            ],
        ),
        out_shape=[jax.ShapeDtypeStruct((4, 1024, 256), BF16)] * 2,
        compiler_params=pltpu.CompilerParams(vmem_limit_bytes=VMEM_BYTES),
        cost_estimate=pl.CostEstimate(flops=10**7, bytes_accessed=2**20, transcendentals=0),
        name="mixed",
    )(me, lengths, skip, active, cum, size, init, gate, gain, weight)


def plan_kernel(me_ref, hit_off_ref, hit_row_ref, store_ref, *refs):
    base_refs, plan_ref = refs[:WINDOW], refs[WINDOW]
    me = me_ref[0]
    count = 512
    offs = store_ref[...]
    item = lax.broadcasted_iota(jnp.int32, (1, count), 1)
    source = item >> 4
    owner = (source + offs) & 31
    nearby = (owner + 32 - me) & 31
    base = jnp.zeros((1, count), jnp.int32)
    for n in range(WINDOW):
        base = jnp.where(nearby == n, base_refs[n][0], base)
    row = lax.broadcasted_iota(jnp.int32, (count, count), 0)
    col = lax.broadcasted_iota(jnp.int32, (count, count), 1)
    before = row < col
    together = (row >> 4) == (col >> 4)

    def ones(mask):
        return jnp.where(mask, 1.0, 0.0).astype(BF16)

    owned = lax.broadcasted_iota(jnp.int32, (32, count), 0) == owner
    ranks = jnp.dot(ones(owned), ones(before), preferred_element_type=F32)
    rank = jnp.sum(jnp.where(owned, ranks, 0.0), axis=0, keepdims=True).astype(jnp.int32)
    distance = lax.broadcasted_iota(jnp.int32, (16, count), 0)
    alike = ones(distance == offs)
    inside = jnp.dot(alike, ones(before & together), preferred_element_type=F32)
    total = jnp.dot(alike, ones(together), preferred_element_type=F32)
    place = jnp.sum(
        jnp.where(distance == offs, inside, 0.0) + jnp.where(distance > offs, total, 0.0),
        axis=0,
        keepdims=True,
    ).astype(jnp.int32)
    target = (base + rank) & 15
    code = (1 + offs * 16 + place).astype(F32)
    key = jnp.where((rank < 16) & (nearby < WINDOW), owner * 16 + target, -1)
    number = lax.broadcasted_iota(jnp.int32, (32, count), 0)
    wanted = me * 16 + number
    for b in range(WINDOW):
        asker = (me + 32 - b) & 31
        for j in range(4):
            slot = asker * 2 + j // 2
            place_wanted = ((asker + hit_off_ref[j % 2, slot]) & 31) * 16 + hit_row_ref[j % 2, slot]
            wanted = jnp.where(number == 16 + 4 * b + j, place_wanted, wanted)
    found = jnp.sum(jnp.where(wanted == key, code, 0.0), axis=1, keepdims=True)
    plan_ref[...] = jnp.broadcast_to(found, (32, 128)).astype(jnp.int32)


def make_plan(me, hit_off, hit_row, store_row, bases):
    smem = pl.BlockSpec(memory_space=pltpu.SMEM)
    return pl.pallas_call(
        plan_kernel,
        in_specs=[smem, smem, smem, pl.BlockSpec(memory_space=pltpu.VMEM)] + [smem] * WINDOW,
        out_specs=pl.BlockSpec(memory_space=pltpu.VMEM),
        out_shape=jax.ShapeDtypeStruct((32, 128), jnp.int32),
        compiler_params=pltpu.CompilerParams(vmem_limit_bytes=VMEM_BYTES),
        name="plan",
    )(me, hit_off, hit_row, store_row, *bases)


def asked(plan_ref, hit_off_ref, hit_row_ref, me, back):
    asker = (me + 32 - back) & 31
    deltas, numbers, places, rows, founds = [], [], [], [], []
    for j in range(4):
        slot = asker * 2 + j // 2
        off = hit_off_ref[j % 2, slot]
        code = plan_ref[16 + 4 * back + j, 0]
        found = code > 0
        delta = off - jnp.where(found, (code - 1) >> 4, 0)
        number = jnp.int32(0)
        for other in deltas:
            number = number + (other == delta).astype(jnp.int32)
        deltas.append(delta)
        numbers.append(number)
        places.append((code - 1) & 15)
        rows.append(hit_row_ref[j % 2, slot])
        founds.append(found)
    return deltas, numbers, places, rows, founds


def start_from(pieces, place, start):
    for piece, begin, end in pieces:

        @pl.when((place >= begin) & (place < end))
        def _():
            start(piece, place - begin)


def serve_kernel(me_ref, plan_ref, hit_off_ref, hit_row_ref, *refs):
    pieces = [(refs[n], CUTS[n], CUTS[n + 1]) for n in range(len(SIZES))]
    pool_ref, pool_conv_ref, far_ref, near_ref = refs[len(SIZES) : len(SIZES) + 4]
    lines, tail, packed, jobs, sems, tail_sems = refs[len(SIZES) + 4 :]
    lines[...] = pool_conv_ref[...].astype(F32)
    tail[18:32, :] = jnp.zeros((14, 128), F32)
    for d in range(1, WINDOW):
        deltas, numbers, places, rows, founds = asked(
            plan_ref, hit_off_ref, hit_row_ref, me_ref[0], d
        )
        for j in range(4):
            wanted = (deltas[j] == d) & (numbers[j] < DOWN[d - 1])
            jobs[0, 4 * d + j] = jnp.where(wanted, jnp.where(founds[j], 1, 2), 0)
            jobs[1, 4 * d + j] = jnp.minimum(numbers[j], DOWN[d - 1] - 1)
            jobs[2, 4 * d + j] = jnp.where(founds[j], places[j], rows[j])

    for d in range(1, WINDOW):
        out, begin = ((near_ref, 0), (far_ref, DOWN[2]), (far_ref, 0))[d - 1]

        def dest(n):
            return out.at[begin + jobs[1, n]]

        def state(n):
            return pltpu.make_async_copy(
                pool_ref.at[jobs[2, n]], dest(n).at[pl.ds(0, STATE_ROWS)], sems.at[n]
            )

        def rest(n):
            return pltpu.make_async_copy(
                packed.at[n], dest(n).at[pl.ds(STATE_ROWS, TAIL_ROWS)], tail_sems.at[n]
            )

        def begin_job(j, carry):
            n = 4 * d + j

            @pl.when(jobs[0, n] == 1)
            def _():
                start_from(
                    pieces,
                    jobs[2, n],
                    lambda piece, row: pltpu.make_async_copy(
                        piece.at[row], dest(n), sems.at[n]
                    ).start(),
                )

            @pl.when(jobs[0, n] == 2)
            def _():
                state(n).start()
                for r in range(3):
                    line = lines[r, pl.ds(jobs[2, n], 1), :]
                    for c in range(6):
                        tail[r * 6 + c : r * 6 + c + 1, :] = line[:, 128 * c : 128 * (c + 1)]
                packed[n] = tail[...].astype(BF16)
                rest(n).start()

            return carry

        def end_job(j, carry):
            n = 4 * d + j

            @pl.when(jobs[0, n] == 1)
            def _():
                pltpu.make_async_copy(pieces[0][0].at[0], dest(n), sems.at[n]).wait()

            @pl.when(jobs[0, n] == 2)
            def _():
                state(n).wait()
                rest(n).wait()

            return carry

        lax.fori_loop(0, 4, begin_job, 0)
        lax.fori_loop(0, 4, end_job, 0)


def serve(me, plan, hit_off, hit_row, pieces, pool, pool_conv):
    smem = pl.BlockSpec(memory_space=pltpu.SMEM)
    hbm = pl.BlockSpec(memory_space=pl.ANY)
    vmem = pl.BlockSpec(memory_space=pltpu.VMEM)
    return pl.pallas_call(
        serve_kernel,
        in_specs=[smem] * 4 + [hbm] * (len(SIZES) + 1) + [vmem],
        out_specs=[vmem] * 2,
        out_shape=[
            jax.ShapeDtypeStruct((DOWN[1] + DOWN[2], ITEM_ROWS, 128), BF16),
            jax.ShapeDtypeStruct((DOWN[0], ITEM_ROWS, 128), BF16),
        ],
        scratch_shapes=[
            pltpu.VMEM((3, 16, 768), F32),
            pltpu.VMEM((TAIL_ROWS, 128), F32),
            pltpu.VMEM((16, TAIL_ROWS, 128), BF16),
            pltpu.SMEM((3, 16), jnp.int32),
            pltpu.SemaphoreType.DMA((16,)),
            pltpu.SemaphoreType.DMA((16,)),
        ],
        compiler_params=pltpu.CompilerParams(vmem_limit_bytes=VMEM_BYTES),
        name="serve",
    )(me, plan, hit_off, hit_row, *pieces, pool, pool_conv)


def settle_kernel(layout, me_ref, plan_ref, hit_off_ref, hit_row_ref, *refs):
    count = len(layout)
    by_hop = [
        [(refs[n], begin, end) for n, (at, begin, end) in enumerate(layout) if at == hop]
        for hop in range(WINDOW)
    ]
    one_ref, two_ref, three_ref, pool_ref, pool_conv_ref = refs[count : count + 5]
    terms = refs[count + 5 : count + 9]
    pool_out, pool_conv_out, next_out, next_conv_out, mixed_out = refs[count + 9 : count + 14]
    lines, next_lines, tails, wide, held, sems, tail_sems, term_sems = refs[count + 14 :]

    def state_of(source, dest, n):
        return pltpu.make_async_copy(source, dest, sems.at[n])

    def tail_of(source, n):
        return pltpu.make_async_copy(source, tails.at[n], tail_sems.at[n])

    def start_item(array, index, dest, n):
        state_of(array.at[index, pl.ds(0, STATE_ROWS)], dest, n).start()
        tail_of(array.at[index, pl.ds(STATE_ROWS, TAIL_ROWS)], n).start()

    def from_items(hop, place, dest, n):
        for at, pieces in enumerate(by_hop):

            @pl.when(hop == at)
            def _():
                start_from(pieces, place, lambda piece, row: start_item(piece, row, dest, n))

    def begin_row(n, carry):
        code = plan_ref[n, 0]

        @pl.when(code == 0)
        def _():
            state_of(pool_ref.at[n], pool_out.at[n], n).start()

        @pl.when(code > 0)
        def _():
            from_items((code - 1) >> 4, (code - 1) & 15, pool_out.at[n], n)

        return carry

    def term(n):
        return pltpu.make_async_copy(terms[n], held.at[n], term_sems.at[n])

    for n in range(4):
        term(n).start()
    lax.fori_loop(0, ITEMS, begin_row, 0)

    deltas, numbers, places, rows, founds = asked(
        plan_ref, hit_off_ref, hit_row_ref, me_ref[0], 0
    )
    kept = []
    for j in range(4):
        n = ITEMS + j
        dest = next_out.at[j % 2, j // 2]
        here = jnp.logical_not(founds[j]) & (deltas[j] == 0)
        kept.append(here)

        @pl.when(here)
        def _():
            state_of(pool_ref.at[rows[j]], dest, n).start()

        @pl.when(founds[j] & (deltas[j] <= 0))
        def _():
            from_items(-deltas[j], places[j], dest, n)

        for d in range(1, WINDOW):
            array, begin = ((one_ref, 0), (two_ref, DOWN[2]), (three_ref, 0))[d - 1]

            @pl.when(deltas[j] == d)
            def _():
                start_item(array, begin + jnp.minimum(numbers[j], DOWN[d - 1] - 1), dest, n)

    lines[...] = pool_conv_ref[...].astype(F32)
    some_tail = three_ref.at[0, pl.ds(STATE_ROWS, TAIL_ROWS)]

    for j in range(4):
        n = ITEMS + j

        @pl.when(kept[j])
        def _():
            for r in range(3):
                next_lines[j % 2, r, j // 2 : j // 2 + 1, :] = lines[r, pl.ds(rows[j], 1), :]

        @pl.when(jnp.logical_not(kept[j]))
        def _():
            tail_of(some_tail, n).wait()
            tail = tails[n].astype(F32)
            for r in range(3):
                for c in range(6):
                    next_lines[j % 2, r, j // 2 : j // 2 + 1, 128 * c : 128 * (c + 1)] = tail[
                        r * 6 + c : r * 6 + c + 1
                    ]

    def end_tail(n, carry):
        @pl.when(plan_ref[n, 0] > 0)
        def _():
            tail_of(some_tail, n).wait()

        return carry

    lax.fori_loop(0, ITEMS, end_tail, 0)
    wide[...] = tails[0:ITEMS].astype(F32)
    stored = jnp.zeros((ITEMS, 128), jnp.int32)
    row = lax.broadcasted_iota(jnp.int32, (ITEMS, 128), 0)
    for n in range(ITEMS):
        stored = jnp.where(row == n, plan_ref[n, 0], stored)
    for r in range(3):
        for c in range(6):
            cols = slice(128 * c, 128 * (c + 1))
            lines[r, :, cols] = jnp.where(stored > 0, wide[:, r * 6 + c, :], lines[r, :, cols])

    for n in range(4):
        term(n).wait()

    def add(n, carry):
        part = pl.ds(pl.multiple_of(n * 128, 128), 128)
        total = held[0, part, :].astype(F32)
        for k in range(1, 4):
            total = total + held[k, part, :].astype(F32)
        mixed_out[part, :] = total.astype(BF16)
        return carry

    lax.fori_loop(0, 8, add, 0)
    pool_conv_out[...] = lines[...].astype(BF16)
    next_conv_out[...] = next_lines[...].astype(BF16)
    def end_row(n, carry):
        state_of(pool_ref.at[0], pool_out.at[n], n).wait()
        return carry

    lax.fori_loop(0, ITEMS, end_row, 0)
    for j in range(4):
        state_of(pool_ref.at[0], next_out.at[j % 2, j // 2], ITEMS + j).wait()


def settle(layout, me, plan, hit_off, hit_row, received, down, pool, pool_conv, terms):
    smem = pl.BlockSpec(memory_space=pltpu.SMEM)
    hbm = pl.BlockSpec(memory_space=pl.ANY)
    vmem = pl.BlockSpec(memory_space=pltpu.VMEM)
    return pl.pallas_call(
        functools.partial(settle_kernel, layout),
        in_specs=[smem] * 4 + [hbm] * (len(layout) + 4) + [vmem] + [hbm] * 4,
        out_specs=[vmem] * 5,
        out_shape=[
            jax.ShapeDtypeStruct((16, STATE_ROWS, 128), BF16),
            jax.ShapeDtypeStruct((3, 16, 768), BF16),
            jax.ShapeDtypeStruct((2, 2, STATE_ROWS, 128), BF16),
            jax.ShapeDtypeStruct((2, 3, 2, 768), BF16),
            jax.ShapeDtypeStruct((1024, 256), BF16),
        ],
        scratch_shapes=[
            pltpu.VMEM((3, 16, 768), F32),
            pltpu.VMEM((2, 3, 2, 768), F32),
            pltpu.VMEM((ITEMS + 4, TAIL_ROWS, 128), BF16),
            pltpu.VMEM((ITEMS, TAIL_ROWS, 128), F32),
            pltpu.VMEM((4, 1024, 256), BF16),
            pltpu.SemaphoreType.DMA((ITEMS + 4,)),
            pltpu.SemaphoreType.DMA((ITEMS + 4,)),
            pltpu.SemaphoreType.DMA((4,)),
        ],
        compiler_params=pltpu.CompilerParams(vmem_limit_bytes=VMEM_BYTES),
        name="settle",
    )(me, plan, hit_off, hit_row, *received, *down, pool, pool_conv, *terms)


def after(value, *others):
    return lax.optimization_barrier((value,) + others)[0]


def body(
    conv_input,
    conv_weight,
    conv_bias,
    step_raw,
    step_bias,
    decay_log,
    skip_weight,
    gate_input,
    norm_gain,
    out_weight,
    ssm_state,
    conv_state,
    pool_ssm,
    pool_conv,
    lengths,
    store_offset,
    store_base,
    hit_offset,
    hit_row,
):
    me = jnp.stack([lax.axis_index("cache"), lax.axis_index("tp")]).astype(jnp.int32)
    offsets = jnp.transpose(store_offset, (1, 2, 0)).reshape(8, 64)
    hit_off = jnp.transpose(hit_offset, (1, 2, 0)).reshape(2, 64)
    hit_at = hit_row.T
    init = ssm_state.reshape(2, 2, STATE_ROWS, 128)
    pool = pool_ssm.reshape(16, STATE_ROWS, 128)
    pool_lines = jnp.transpose(pool_conv, (1, 2, 0, 3)).reshape(3, 16, 768)
    conv_lines = jnp.transpose(conv_state, (0, 2, 3, 1, 4)).reshape(2, 3, 2, 768)

    active, cum, size, more, *pieces = make_states(
        me,
        offsets,
        lengths,
        step_bias,
        decay_log,
        conv_input.reshape(2, 2, 256, 768),
        conv_lines,
        conv_weight.reshape(2, 4, 768),
        conv_bias,
        step_raw,
        init,
    )
    first = [passed_along(piece, 1) for piece in pieces[:3]]
    base = after(store_base, *pieces)
    bases = [base if n == 0 else passed_along(base, -n) for n in range(WINDOW)]
    plan = make_plan(me, hit_off, hit_at, store_offset.reshape(1, 512), bases)
    served, near = serve(me, plan, hit_off, hit_at, pieces, pool, pool_lines)
    down = passed_along(served, -1)
    mine, theirs = make_mixed(
        me,
        lengths,
        skip_weight,
        after(active, served),
        cum,
        size,
        init,
        gate_input,
        norm_gain,
        out_weight,
    )
    first, down, near, mine, theirs = lax.optimization_barrier((first, down, near, mine, theirs))

    second = passed_along(first[0], 1)
    two = passed_along(down, -1)
    other = lax.ppermute(theirs, "tp", [(i, i ^ 1) for i in range(8)])
    sums = [(mine[away].astype(F32) + other[away].astype(F32)).astype(BF16) for away in range(4)]

    def to_chip(away):
        return lax.ppermute(sums[away], "tp", [(i, (i + 2 * away) % 8) for i in range(8)])

    def if_needed(needed, part):
        return lax.cond(needed, lambda part: passed_along(part, 1), lambda part: part, part)

    def follow(parts):
        late = passed_along(parts[0], 1)
        return [late, passed_along(late, 1), passed_along(parts[1], 1)]

    parts = [to_chip(1), to_chip(3)]
    extra = lax.cond(
        more[0] > 0,
        follow,
        lambda parts: [parts[0], parts[0], parts[1]],
        [pieces[3], first[2]],
    )
    behind = if_needed(more[1] > 0, after(first[1], sums[0], extra[0]))
    second, behind, two, parts, extra, sums, near = lax.optimization_barrier(
        (second, behind, two, parts, extra, sums, near)
    )

    third = passed_along(second[: THIRD[0]], 1)
    three, one = passed_along(two[: DOWN[2]], -1), passed_along(near, -1)
    terms = [sums[0], *parts, to_chip(2)]
    fourth = if_needed(more[2] > 0, second[THIRD[0] : THIRD[1]])
    layout = [(0, begin, end) for begin, end in zip(CUTS, CUTS[1:])]
    layout += [(1, begin, end) for begin, end in zip(CUTS[:3], CUTS[1:4])]
    layout += [(2, 0, 8), (2, 8, 12), (3, 0, THIRD[0]), (3, *THIRD)]
    layout += [(1, 14, 16), (2, 14, 16), (2, 12, 14)]
    pool_out, pool_lines_out, next_ssm, next_lines, mixed = settle(
        layout,
        me,
        plan,
        hit_off,
        hit_at,
        [*pieces, *first, second, behind, third, fourth, *extra],
        [one, two, three],
        pool,
        pool_lines,
        terms,
    )
    return (
        mixed.reshape(2, 2, 256, 256),
        pool_out.reshape(pool_ssm.shape),
        jnp.transpose(pool_lines_out.reshape(3, 1, 16, 768), (2, 0, 1, 3)),
        next_ssm.reshape(ssm_state.shape),
        jnp.transpose(next_lines.reshape(2, 3, 1, 2, 768), (0, 3, 1, 2, 4)),
    )


def solution(mesh):
    in_specs = (
        P(None, "cache", None, "tp", None),
        P(None, None, "tp", None),
        P(None, "tp", None),
        P(None, "cache", "tp", None),
        P(None, "tp"),
        P(None, "tp"),
        P(None, "tp"),
        P(None, "cache", None, "tp"),
        P(None, "tp"),
        P(None, "tp", None),
        P(None, "cache", "tp", None, None),
        P(None, "cache", None, "tp", None),
        P("cache", "tp", None, None),
        P("cache", None, "tp", None),
        P("cache"),
        P(),
        P("cache"),
        P(),
        P(),
    )
    out_specs = (
        P(None, "cache", None, "tp"),
        P("cache", "tp", None, None),
        P("cache", None, "tp", None),
        P(None, "cache", "tp", None, None),
        P(None, "cache", None, "tp", None),
    )
    return jax.shard_map(body, mesh=mesh, in_specs=in_specs, out_specs=out_specs, check_vma=False)
```

```python
import functools

import jax
import jax.numpy as jnp
from jax import lax
from jax.experimental import pallas as pl
from jax.experimental.pallas import tpu as pltpu
from jax.sharding import PartitionSpec as P

BOUNDS = 4
WINDOW = 4
EPS = 1e-05
STATE_ROWS = 512
ITEM_ROWS = 544
TAIL_ROWS = 32
ITEMS = 16
VMEM_BYTES = 60 * 2**20
F32 = jnp.float32
BF16 = jnp.bfloat16
CUTS = (0, 8, 12, 14, 16)
SIZES = tuple(end - begin for begin, end in zip(CUTS, CUTS[1:]))
THIRD = (5, 8)
DOWN = (4, 4, 2)


def passed_along(array, by):
    size = lax.axis_size("cache")
    return lax.ppermute(array, "cache", [(i, (i + by) % size) for i in range(size)])


def silu(v):
    return 0.5 * v * (1.0 + jnp.tanh(0.5 * v))


def states_kernel(
    me_ref,
    offset_ref,
    length_ref,
    bias_ref,
    decay_ref,
    offsets_ref,
    conv_in_ref,
    conv_state_ref,
    taps_ref,
    shift_ref,
    step_ref,
    init_ref,
    active_ref,
    cum_ref,
    size_ref,
    more_ref,
    *refs,
):
    pieces = refs[: len(SIZES)]
    ext, tail, held, sems = refs[len(SIZES) :]
    turn = pl.program_id(0)

    @pl.when(turn == 0)
    def _():
        offsets = offsets_ref[...]
        even = lax.broadcasted_iota(jnp.int32, (1, 64), 1) % 2 == 0
        far = []
        for n in range(1, WINDOW):
            of_slot = jnp.sum(jnp.where(offsets >= n, 1.0, 0.0), axis=0, keepdims=True)
            after_it = jnp.concatenate([of_slot[:, 1:], of_slot[:, :1]], axis=1)
            far.append(jnp.max(jnp.where(even, of_slot + after_it, 0.0)).astype(jnp.int32))
        more_ref[0] = ((far[0] > CUTS[3]) | (far[1] > CUTS[2])).astype(jnp.int32)
        more_ref[1] = (far[1] > CUTS[1]).astype(jnp.int32)
        more_ref[2] = (far[2] > THIRD[0]).astype(jnp.int32)

    slot, layer = turn // 2, turn % 2
    half = turn % 2

    first = me_ref[0] * 2
    offs = [offset_ref[n % 8, first + n // 8] for n in range(ITEMS)]
    places = []
    for k in range(BOUNDS):
        own = offset_ref[layer * BOUNDS + k, first + slot]
        number = turn_item = slot * 8 + layer * BOUNDS + k
        place = jnp.int32(0)
        for n in range(ITEMS):
            ahead = (offs[n] > own) | ((offs[n] == own) & (n < turn_item))
            place = place + ahead.astype(jnp.int32)
        places.append(place)

    def wait(which, k):
        pltpu.make_async_copy(held.at[which, k], pieces[0].at[0], sems.at[which, k]).wait()

    before = conv_state_ref[0].astype(F32)
    ext[5:8, :] = jnp.where(slot == 0, before[:, 0, :], before[:, 1, :])
    ext[8:264, :] = conv_in_ref[0, 0].astype(F32)
    taps = taps_ref[0].astype(F32)
    shift = shift_ref[0]
    for c in range(6):
        cols = slice(128 * c, 128 * (c + 1))
        summed = shift[:, cols]
        for k in range(4):
            summed = summed + taps[k : k + 1, cols] * ext[5 + k : 261 + k, cols]
        active_ref[0, :, cols] = silu(summed).astype(BF16)

    rows = lax.broadcasted_iota(jnp.int32, (8, 256), 0)
    bias = jnp.zeros((8, 256), F32)
    rate = jnp.zeros((8, 256), F32)
    for h in range(8):
        bias = jnp.where(rows == h, bias_ref[layer, h], bias)
        rate = jnp.where(rows == h, decay_ref[layer, h], rate)
    raw = step_ref[0, 0].astype(F32) + bias
    soft = jnp.maximum(raw, 0.0) + jnp.log1p(jnp.exp(-jnp.abs(raw)))
    here = lax.broadcasted_iota(jnp.int32, (8, 256), 1) < length_ref[slot]
    size = jnp.where(here, soft, 0.0)
    drop = size * (-jnp.exp(rate))
    hi = drop.astype(BF16)
    rest = drop - hi.astype(F32)
    mid = rest.astype(BF16)
    low = (rest - mid.astype(F32)).astype(BF16)
    upto = (
        lax.broadcasted_iota(jnp.int32, (256, 256), 0)
        <= lax.broadcasted_iota(jnp.int32, (256, 256), 1)
    ).astype(F32).astype(BF16)
    cum = (
        jnp.dot(low, upto, preferred_element_type=F32)
        + jnp.dot(mid, upto, preferred_element_type=F32)
        + jnp.dot(hi, upto, preferred_element_type=F32)
    )
    cum_ref[0] = cum
    size_ref[0] = size

    lane = lax.broadcasted_iota(jnp.int32, (8, 256), 1)
    ends = [cum[:, 64 * k + 63 : 64 * k + 64] for k in range(BOUNDS)]
    last = ends[3]
    for k in (2, 1, 0):
        last = jnp.where(lane < 64 * (k + 1), ends[k], last)
    share = jnp.exp(last - cum) * size
    fade = [jnp.exp(ends[0])] + [jnp.exp(ends[k] - ends[k - 1]) for k in range(1, BOUNDS)]
    x_turned = active_ref[0, :, 0:512].astype(F32).T
    b_rows = active_ref[0, :, 512:640]
    row = lax.broadcasted_iota(jnp.int32, (128, 128), 0)
    pairs = []
    for p in range(2):
        b_here = b_rows[128 * p : 128 * (p + 1)]
        zero = jnp.zeros_like(b_here)
        pairs.append(
            jnp.concatenate(
                [jnp.where(row < 64, b_here, zero), jnp.where(row < 64, zero, b_here)], axis=1
            )
        )

    @pl.when(turn >= 2)
    def _():
        for k in range(BOUNDS):
            wait(half, k)

    for h in range(8):
        part = slice(64 * h, 64 * (h + 1))
        scaled = (x_turned[part] * share[h : h + 1]).astype(BF16)
        grown = [
            jnp.dot(scaled[:, 128 * p : 128 * (p + 1)], pairs[p], preferred_element_type=F32)
            for p in range(2)
        ]
        state = init_ref[0, 0, part, :].astype(F32)
        for k in range(BOUNDS):
            more = grown[k // 2][:, 128 * (k % 2) : 128 * (k % 2 + 1)]
            state = state * fade[k][h : h + 1] + more
            held[half, k, part, :] = state.astype(BF16)

    for k in range(BOUNDS):
        start = jnp.minimum(length_ref[slot], 64 * (k + 1)) + 5
        for r in range(3):
            line = ext[pl.ds(start + r, 1), :]
            for c in range(6):
                tail[r * 6 + c : r * 6 + c + 1, :] = line[:, 128 * c : 128 * (c + 1)]
        tail[18:32, :] = jnp.zeros((14, 128), F32)
        held[half, k, STATE_ROWS:ITEM_ROWS, :] = tail[...].astype(BF16)

    for k in range(BOUNDS):
        for n, piece in enumerate(pieces):

            @pl.when((places[k] >= CUTS[n]) & (places[k] < CUTS[n + 1]))
            def _():
                pltpu.make_async_copy(
                    held.at[half, k], piece.at[places[k] - CUTS[n]], sems.at[half, k]
                ).start()

    @pl.when(turn == 3)
    def _():
        for which in range(2):
            for k in range(BOUNDS):
                wait(which, k)


def make_states(me, offsets, lengths, step_bias, decay_log, conv_in, conv_state, taps, shift, step, init):
    return pl.pallas_call(
        states_kernel,
        grid_spec=pltpu.PrefetchScalarGridSpec(
            num_scalar_prefetch=5,
            grid=(4,),
            in_specs=[
                pl.BlockSpec((8, 64), lambda g, *_: (0, 0)),
                pl.BlockSpec((1, 1, 256, 768), lambda g, *_: (g % 2, g // 2, 0, 0)),
                pl.BlockSpec((1, 3, 2, 768), lambda g, *_: (g % 2, 0, 0, 0)),
                pl.BlockSpec((1, 4, 768), lambda g, *_: (g % 2, 0, 0)),
                pl.BlockSpec((1, 1, 768), lambda g, *_: (g % 2, 0, 0)),
                pl.BlockSpec((1, 1, 8, 256), lambda g, *_: (g % 2, g // 2, 0, 0)),
                pl.BlockSpec((1, 1, 512, 128), lambda g, *_: (g % 2, g // 2, 0, 0)),
            ],
            out_specs=[
                pl.BlockSpec((1, 256, 768), lambda g, *_: (g, 0, 0)),
                pl.BlockSpec((1, 8, 256), lambda g, *_: (g, 0, 0)),
                pl.BlockSpec((1, 8, 256), lambda g, *_: (g, 0, 0)),
                pl.BlockSpec(memory_space=pltpu.SMEM),
            ]
            + [pl.BlockSpec(memory_space=pl.ANY)] * len(SIZES),
            scratch_shapes=[
                pltpu.VMEM((264, 768), F32),
                pltpu.VMEM((TAIL_ROWS, 128), F32),
                pltpu.VMEM((2, BOUNDS, ITEM_ROWS, 128), BF16),
                pltpu.SemaphoreType.DMA((2, BOUNDS)),
            ],
        ),
        out_shape=[
            jax.ShapeDtypeStruct((4, 256, 768), BF16),
            jax.ShapeDtypeStruct((4, 8, 256), F32),
            jax.ShapeDtypeStruct((4, 8, 256), F32),
            jax.ShapeDtypeStruct((3,), jnp.int32),
        ]
        + [jax.ShapeDtypeStruct((rows, ITEM_ROWS, 128), BF16) for rows in SIZES],
        compiler_params=pltpu.CompilerParams(vmem_limit_bytes=VMEM_BYTES),
        cost_estimate=pl.CostEstimate(flops=10**9, bytes_accessed=8 * 2**20, transcendentals=10**6),
        name="states",
    )(me, offsets, lengths, step_bias, decay_log, offsets, conv_in, conv_state, taps, shift, step, init)


def mixed_kernel(
    me_ref,
    length_ref,
    skip_ref,
    active_ref,
    cum_ref,
    size_ref,
    init_ref,
    gate_ref,
    gain_ref,
    weight_ref,
    mine_ref,
    theirs_ref,
    gated,
    carried,
    scores,
    columns,
):
    layer, slot = pl.program_id(0) // 2, pl.program_id(0) % 2
    chip, core = me_ref[1] >> 1, me_ref[1] & 1
    b_rows = active_ref[0, :, 512:640]
    c_rows = active_ref[0, :, 640:768]
    nt = (((1,), (1,)), ((), ()))
    scores[...] = lax.dot_general(c_rows, b_rows, nt, preferred_element_type=F32)
    carried[...] = lax.dot_general(c_rows, init_ref[0, 0], nt, preferred_element_type=F32)
    turned = jnp.concatenate([cum_ref[0], jnp.zeros((120, 256), F32)], axis=0).T
    for h in range(8):
        columns[h] = turned[:, h : h + 1]
    low_lane = lax.broadcasted_iota(jnp.int32, (256, 128), 1) < 64
    causal = lax.broadcasted_iota(jnp.int32, (128, 128), 0) >= lax.broadcasted_iota(
        jnp.int32, (128, 128), 1
    )

    def pair(p, squares):
        cols = pl.ds(pl.multiple_of(128 * p, 128), 128)
        x_pair = active_ref[0, :, cols]
        halves = []
        for h in (2 * p, 2 * p + 1):
            row_cum = cum_ref[0, pl.ds(h, 1), :]
            row_size = size_ref[0, pl.ds(h, 1), :]
            col = columns[h]
            top = jnp.where(causal, jnp.exp(jnp.where(causal, col[:128] - row_cum[:, :128], 0.0)), 0.0)
            top = (scores[:128, :128] * top * row_size[:, :128]).astype(BF16)
            left = jnp.exp(col[128:] - row_cum[:, :128])
            left = (scores[128:, :128] * left * row_size[:, :128]).astype(BF16)
            right = jnp.where(causal, jnp.exp(jnp.where(causal, col[128:] - row_cum[:, 128:], 0.0)), 0.0)
            right = (scores[128:, 128:] * right * row_size[:, 128:]).astype(BF16)
            upper = jnp.dot(top, x_pair[:128], preferred_element_type=F32)
            lower = jnp.dot(
                jnp.concatenate([left, right], axis=1), x_pair, preferred_element_type=F32
            )
            halves.append(jnp.concatenate([upper, lower], axis=0))
        inner = jnp.where(low_lane, halves[0], halves[1])
        growth = jnp.exp(jnp.where(low_lane, columns[2 * p], columns[2 * p + 1]))
        skip = jnp.where(low_lane, skip_ref[layer, 2 * p], skip_ref[layer, 2 * p + 1])
        output = inner + carried[:, cols] * growth + skip * x_pair.astype(F32)
        product = output * silu(gate_ref[0, 0, :, cols].astype(F32))
        gated[:, cols] = product
        return squares + jnp.sum(product * product, axis=1, keepdims=True)

    squares = lax.fori_loop(0, 4, pair, jnp.zeros((256, 1), F32))
    inverse = lax.rsqrt(squares * (1.0 / 512.0) + EPS)
    valid = lax.broadcasted_iota(jnp.int32, (256, 1), 0) < length_ref[slot]
    normed = gated[...] * inverse * gain_ref[pl.ds(layer, 1), :]
    normed = jnp.where(valid, normed, 0.0).astype(BF16)

    def block(away, carry):
        for out_ref, its_core in ((mine_ref, core), (theirs_ref, 1 - core)):
            at = pl.multiple_of((((chip + away) & 3) * 2 + its_core) * 256, 256)
            out_ref[away] = jnp.dot(
                normed, weight_ref[0, :, pl.ds(at, 256)], preferred_element_type=F32
            ).astype(BF16)
        return carry

    lax.fori_loop(0, 4, block, 0)


def make_mixed(me, lengths, skip, active, cum, size, init, gate, gain, weight):
    return pl.pallas_call(
        mixed_kernel,
        grid_spec=pltpu.PrefetchScalarGridSpec(
            num_scalar_prefetch=3,
            grid=(4,),
            in_specs=[
                pl.BlockSpec((1, 256, 768), lambda g, *_: (2 * (g % 2) + g // 2, 0, 0)),
                pl.BlockSpec((1, 8, 256), lambda g, *_: (2 * (g % 2) + g // 2, 0, 0)),
                pl.BlockSpec((1, 8, 256), lambda g, *_: (2 * (g % 2) + g // 2, 0, 0)),
                pl.BlockSpec((1, 1, 512, 128), lambda g, *_: (g // 2, g % 2, 0, 0)),
                pl.BlockSpec((1, 1, 256, 512), lambda g, *_: (g // 2, g % 2, 0, 0)),
                pl.BlockSpec((2, 512), lambda g, *_: (0, 0)),
                pl.BlockSpec((1, 512, 2048), lambda g, *_: (g // 2, 0, 0)),
            ],
            out_specs=[pl.BlockSpec((4, 256, 256), lambda g, *_: (0, g, 0))] * 2,
            scratch_shapes=[
                pltpu.VMEM((256, 512), F32),
                pltpu.VMEM((256, 512), F32),
                pltpu.VMEM((256, 256), F32),
                pltpu.VMEM((8, 256, 1), F32),
            ],
        ),
        out_shape=[jax.ShapeDtypeStruct((4, 1024, 256), BF16)] * 2,
        compiler_params=pltpu.CompilerParams(vmem_limit_bytes=VMEM_BYTES),
        cost_estimate=pl.CostEstimate(flops=10**7, bytes_accessed=2**20, transcendentals=0),
        name="mixed",
    )(me, lengths, skip, active, cum, size, init, gate, gain, weight)


def plan_kernel(me_ref, hit_off_ref, hit_row_ref, store_ref, *refs):
    base_refs, plan_ref = refs[:WINDOW], refs[WINDOW]
    me = me_ref[0]
    count = 512
    offs = store_ref[...]
    item = lax.broadcasted_iota(jnp.int32, (1, count), 1)
    source = item >> 4
    owner = (source + offs) & 31
    nearby = (owner + 32 - me) & 31
    base = jnp.zeros((1, count), jnp.int32)
    for n in range(WINDOW):
        base = jnp.where(nearby == n, base_refs[n][0], base)
    row = lax.broadcasted_iota(jnp.int32, (count, count), 0)
    col = lax.broadcasted_iota(jnp.int32, (count, count), 1)
    before = row < col
    together = (row >> 4) == (col >> 4)

    def ones(mask):
        return jnp.where(mask, 1.0, 0.0).astype(BF16)

    owned = lax.broadcasted_iota(jnp.int32, (32, count), 0) == owner
    ranks = jnp.dot(ones(owned), ones(before), preferred_element_type=F32)
    rank = jnp.sum(jnp.where(owned, ranks, 0.0), axis=0, keepdims=True).astype(jnp.int32)
    distance = lax.broadcasted_iota(jnp.int32, (16, count), 0)
    alike = ones(distance == offs)
    inside = jnp.dot(alike, ones(before & together), preferred_element_type=F32)
    total = jnp.dot(alike, ones(together), preferred_element_type=F32)
    place = jnp.sum(
        jnp.where(distance == offs, inside, 0.0) + jnp.where(distance > offs, total, 0.0),
        axis=0,
        keepdims=True,
    ).astype(jnp.int32)
    target = (base + rank) & 15
    code = (1 + offs * 16 + place).astype(F32)
    key = jnp.where((rank < 16) & (nearby < WINDOW), owner * 16 + target, -1)
    number = lax.broadcasted_iota(jnp.int32, (32, count), 0)
    wanted = me * 16 + number
    for b in range(WINDOW):
        asker = (me + 32 - b) & 31
        for j in range(4):
            slot = asker * 2 + j // 2
            place_wanted = ((asker + hit_off_ref[j % 2, slot]) & 31) * 16 + hit_row_ref[j % 2, slot]
            wanted = jnp.where(number == 16 + 4 * b + j, place_wanted, wanted)
    found = jnp.sum(jnp.where(wanted == key, code, 0.0), axis=1, keepdims=True)
    plan_ref[...] = jnp.broadcast_to(found, (32, 128)).astype(jnp.int32)


def make_plan(me, hit_off, hit_row, store_row, bases):
    smem = pl.BlockSpec(memory_space=pltpu.SMEM)
    return pl.pallas_call(
        plan_kernel,
        in_specs=[smem, smem, smem, pl.BlockSpec(memory_space=pltpu.VMEM)] + [smem] * WINDOW,
        out_specs=pl.BlockSpec(memory_space=pltpu.VMEM),
        out_shape=jax.ShapeDtypeStruct((32, 128), jnp.int32),
        compiler_params=pltpu.CompilerParams(vmem_limit_bytes=VMEM_BYTES),
        name="plan",
    )(me, hit_off, hit_row, store_row, *bases)


def asked(plan_ref, hit_off_ref, hit_row_ref, me, back):
    asker = (me + 32 - back) & 31
    deltas, numbers, places, rows, founds = [], [], [], [], []
    for j in range(4):
        slot = asker * 2 + j // 2
        off = hit_off_ref[j % 2, slot]
        code = plan_ref[16 + 4 * back + j, 0]
        found = code > 0
        delta = off - jnp.where(found, (code - 1) >> 4, 0)
        number = jnp.int32(0)
        for other in deltas:
            number = number + (other == delta).astype(jnp.int32)
        deltas.append(delta)
        numbers.append(number)
        places.append((code - 1) & 15)
        rows.append(hit_row_ref[j % 2, slot])
        founds.append(found)
    return deltas, numbers, places, rows, founds


def start_from(pieces, place, start):
    for piece, begin, end in pieces:

        @pl.when((place >= begin) & (place < end))
        def _():
            start(piece, place - begin)


def serve_kernel(me_ref, plan_ref, hit_off_ref, hit_row_ref, *refs):
    pieces = [(refs[n], CUTS[n], CUTS[n + 1]) for n in range(len(SIZES))]
    pool_ref, pool_conv_ref, far_ref, near_ref = refs[len(SIZES) : len(SIZES) + 4]
    lines, tail, packed, jobs, sems, tail_sems = refs[len(SIZES) + 4 :]
    lines[...] = pool_conv_ref[...].astype(F32)
    tail[18:32, :] = jnp.zeros((14, 128), F32)
    for d in range(1, WINDOW):
        deltas, numbers, places, rows, founds = asked(
            plan_ref, hit_off_ref, hit_row_ref, me_ref[0], d
        )
        for j in range(4):
            wanted = (deltas[j] == d) & (numbers[j] < DOWN[d - 1])
            jobs[0, 4 * d + j] = jnp.where(wanted, jnp.where(founds[j], 1, 2), 0)
            jobs[1, 4 * d + j] = jnp.minimum(numbers[j], DOWN[d - 1] - 1)
            jobs[2, 4 * d + j] = jnp.where(founds[j], places[j], rows[j])

    for d in range(1, WINDOW):
        out, begin = ((near_ref, 0), (far_ref, DOWN[2]), (far_ref, 0))[d - 1]

        def dest(n):
            return out.at[begin + jobs[1, n]]

        def state(n):
            return pltpu.make_async_copy(
                pool_ref.at[jobs[2, n]], dest(n).at[pl.ds(0, STATE_ROWS)], sems.at[n]
            )

        def rest(n):
            return pltpu.make_async_copy(
                packed.at[n], dest(n).at[pl.ds(STATE_ROWS, TAIL_ROWS)], tail_sems.at[n]
            )

        def begin_job(j, carry):
            n = 4 * d + j

            @pl.when(jobs[0, n] == 1)
            def _():
                start_from(
                    pieces,
                    jobs[2, n],
                    lambda piece, row: pltpu.make_async_copy(
                        piece.at[row], dest(n), sems.at[n]
                    ).start(),
                )

            @pl.when(jobs[0, n] == 2)
            def _():
                state(n).start()
                for r in range(3):
                    line = lines[r, pl.ds(jobs[2, n], 1), :]
                    for c in range(6):
                        tail[r * 6 + c : r * 6 + c + 1, :] = line[:, 128 * c : 128 * (c + 1)]
                packed[n] = tail[...].astype(BF16)
                rest(n).start()

            return carry

        def end_job(j, carry):
            n = 4 * d + j

            @pl.when(jobs[0, n] == 1)
            def _():
                pltpu.make_async_copy(pieces[0][0].at[0], dest(n), sems.at[n]).wait()

            @pl.when(jobs[0, n] == 2)
            def _():
                state(n).wait()
                rest(n).wait()

            return carry

        lax.fori_loop(0, 4, begin_job, 0)
        lax.fori_loop(0, 4, end_job, 0)


def serve(me, plan, hit_off, hit_row, pieces, pool, pool_conv):
    smem = pl.BlockSpec(memory_space=pltpu.SMEM)
    hbm = pl.BlockSpec(memory_space=pl.ANY)
    vmem = pl.BlockSpec(memory_space=pltpu.VMEM)
    return pl.pallas_call(
        serve_kernel,
        in_specs=[smem] * 4 + [hbm] * (len(SIZES) + 1) + [vmem],
        out_specs=[vmem] * 2,
        out_shape=[
            jax.ShapeDtypeStruct((DOWN[1] + DOWN[2], ITEM_ROWS, 128), BF16),
            jax.ShapeDtypeStruct((DOWN[0], ITEM_ROWS, 128), BF16),
        ],
        scratch_shapes=[
            pltpu.VMEM((3, 16, 768), F32),
            pltpu.VMEM((TAIL_ROWS, 128), F32),
            pltpu.VMEM((16, TAIL_ROWS, 128), BF16),
            pltpu.SMEM((3, 16), jnp.int32),
            pltpu.SemaphoreType.DMA((16,)),
            pltpu.SemaphoreType.DMA((16,)),
        ],
        compiler_params=pltpu.CompilerParams(vmem_limit_bytes=VMEM_BYTES),
        name="serve",
    )(me, plan, hit_off, hit_row, *pieces, pool, pool_conv)


def settle_kernel(layout, me_ref, plan_ref, hit_off_ref, hit_row_ref, *refs):
    count = len(layout)
    by_hop = [
        [(refs[n], begin, end) for n, (at, begin, end) in enumerate(layout) if at == hop]
        for hop in range(WINDOW)
    ]
    one_ref, late_ref, two_ref, three_ref, pool_ref, pool_conv_ref = refs[count : count + 6]
    terms = refs[count + 6 : count + 10]
    pool_out, pool_conv_out, next_out, next_conv_out, mixed_out = refs[count + 10 : count + 15]
    lines, next_lines, tails, wide, held, sems, tail_sems, term_sems = refs[count + 15 :]

    def state_of(source, dest, n):
        return pltpu.make_async_copy(source, dest, sems.at[n])

    def tail_of(source, n):
        return pltpu.make_async_copy(source, tails.at[n], tail_sems.at[n])

    def start_item(array, index, dest, n):
        state_of(array.at[index, pl.ds(0, STATE_ROWS)], dest, n).start()
        tail_of(array.at[index, pl.ds(STATE_ROWS, TAIL_ROWS)], n).start()

    def from_items(hop, place, dest, n):
        for at, pieces in enumerate(by_hop):

            @pl.when(hop == at)
            def _():
                start_from(pieces, place, lambda piece, row: start_item(piece, row, dest, n))

    def begin_row(n, carry):
        code = plan_ref[n, 0]

        @pl.when(code == 0)
        def _():
            state_of(pool_ref.at[n], pool_out.at[n], n).start()

        @pl.when(code > 0)
        def _():
            from_items((code - 1) >> 4, (code - 1) & 15, pool_out.at[n], n)

        return carry

    def term(n):
        return pltpu.make_async_copy(terms[n], held.at[n], term_sems.at[n])

    for n in range(4):
        term(n).start()
    lax.fori_loop(0, ITEMS, begin_row, 0)

    deltas, numbers, places, rows, founds = asked(
        plan_ref, hit_off_ref, hit_row_ref, me_ref[0], 0
    )
    kept = []
    for j in range(4):
        n = ITEMS + j
        dest = next_out.at[j % 2, j // 2]
        here = jnp.logical_not(founds[j]) & (deltas[j] == 0)
        kept.append(here)

        @pl.when(here)
        def _():
            state_of(pool_ref.at[rows[j]], dest, n).start()

        @pl.when(founds[j] & (deltas[j] <= 0))
        def _():
            from_items(-deltas[j], places[j], dest, n)

        number = jnp.minimum(numbers[j], jnp.where(deltas[j] == 3, DOWN[2], DOWN[0]) - 1)

        @pl.when((deltas[j] == 1) & (number < 2))
        def _():
            start_item(one_ref, number, dest, n)

        @pl.when((deltas[j] == 1) & (number >= 2))
        def _():
            start_item(late_ref, number - 2, dest, n)

        @pl.when(deltas[j] == 2)
        def _():
            start_item(two_ref, DOWN[2] + number, dest, n)

        @pl.when(deltas[j] == 3)
        def _():
            start_item(three_ref, number, dest, n)

    lines[...] = pool_conv_ref[...].astype(F32)
    some_tail = three_ref.at[0, pl.ds(STATE_ROWS, TAIL_ROWS)]

    for j in range(4):
        n = ITEMS + j

        @pl.when(kept[j])
        def _():
            for r in range(3):
                next_lines[j % 2, r, j // 2 : j // 2 + 1, :] = lines[r, pl.ds(rows[j], 1), :]

        @pl.when(jnp.logical_not(kept[j]))
        def _():
            tail_of(some_tail, n).wait()
            tail = tails[n].astype(F32)
            for r in range(3):
                for c in range(6):
                    next_lines[j % 2, r, j // 2 : j // 2 + 1, 128 * c : 128 * (c + 1)] = tail[
                        r * 6 + c : r * 6 + c + 1
                    ]

    def end_tail(n, carry):
        @pl.when(plan_ref[n, 0] > 0)
        def _():
            tail_of(some_tail, n).wait()

        return carry

    lax.fori_loop(0, ITEMS, end_tail, 0)
    wide[...] = tails[0:ITEMS].astype(F32)
    stored = jnp.zeros((ITEMS, 128), jnp.int32)
    row = lax.broadcasted_iota(jnp.int32, (ITEMS, 128), 0)
    for n in range(ITEMS):
        stored = jnp.where(row == n, plan_ref[n, 0], stored)
    for r in range(3):
        for c in range(6):
            cols = slice(128 * c, 128 * (c + 1))
            lines[r, :, cols] = jnp.where(stored > 0, wide[:, r * 6 + c, :], lines[r, :, cols])

    for n in range(4):
        term(n).wait()

    def add(n, carry):
        part = pl.ds(pl.multiple_of(n * 128, 128), 128)
        total = held[0, part, :].astype(F32)
        for k in range(1, 4):
            total = total + held[k, part, :].astype(F32)
        mixed_out[part, :] = total.astype(BF16)
        return carry

    lax.fori_loop(0, 8, add, 0)
    pool_conv_out[...] = lines[...].astype(BF16)
    next_conv_out[...] = next_lines[...].astype(BF16)
    def end_row(n, carry):
        state_of(pool_ref.at[0], pool_out.at[n], n).wait()
        return carry

    lax.fori_loop(0, ITEMS, end_row, 0)
    for j in range(4):
        state_of(pool_ref.at[0], next_out.at[j % 2, j // 2], ITEMS + j).wait()


def settle(layout, me, plan, hit_off, hit_row, received, down, pool, pool_conv, terms):
    smem = pl.BlockSpec(memory_space=pltpu.SMEM)
    hbm = pl.BlockSpec(memory_space=pl.ANY)
    vmem = pl.BlockSpec(memory_space=pltpu.VMEM)
    return pl.pallas_call(
        functools.partial(settle_kernel, layout),
        in_specs=[smem] * 4 + [hbm] * (len(layout) + 5) + [vmem] + [hbm] * 4,
        out_specs=[vmem] * 5,
        out_shape=[
            jax.ShapeDtypeStruct((16, STATE_ROWS, 128), BF16),
            jax.ShapeDtypeStruct((3, 16, 768), BF16),
            jax.ShapeDtypeStruct((2, 2, STATE_ROWS, 128), BF16),
            jax.ShapeDtypeStruct((2, 3, 2, 768), BF16),
            jax.ShapeDtypeStruct((1024, 256), BF16),
        ],
        scratch_shapes=[
            pltpu.VMEM((3, 16, 768), F32),
            pltpu.VMEM((2, 3, 2, 768), F32),
            pltpu.VMEM((ITEMS + 4, TAIL_ROWS, 128), BF16),
            pltpu.VMEM((ITEMS, TAIL_ROWS, 128), F32),
            pltpu.VMEM((4, 1024, 256), BF16),
            pltpu.SemaphoreType.DMA((ITEMS + 4,)),
            pltpu.SemaphoreType.DMA((ITEMS + 4,)),
            pltpu.SemaphoreType.DMA((4,)),
        ],
        compiler_params=pltpu.CompilerParams(vmem_limit_bytes=VMEM_BYTES),
        name="settle",
    )(me, plan, hit_off, hit_row, *received, *down, pool, pool_conv, *terms)


def after(value, *others):
    return lax.optimization_barrier((value,) + others)[0]


def body(
    conv_input,
    conv_weight,
    conv_bias,
    step_raw,
    step_bias,
    decay_log,
    skip_weight,
    gate_input,
    norm_gain,
    out_weight,
    ssm_state,
    conv_state,
    pool_ssm,
    pool_conv,
    lengths,
    store_offset,
    store_base,
    hit_offset,
    hit_row,
):
    me = jnp.stack([lax.axis_index("cache"), lax.axis_index("tp")]).astype(jnp.int32)
    offsets = jnp.transpose(store_offset, (1, 2, 0)).reshape(8, 64)
    hit_off = jnp.transpose(hit_offset, (1, 2, 0)).reshape(2, 64)
    hit_at = hit_row.T
    init = ssm_state.reshape(2, 2, STATE_ROWS, 128)
    pool = pool_ssm.reshape(16, STATE_ROWS, 128)
    pool_lines = jnp.transpose(pool_conv, (1, 2, 0, 3)).reshape(3, 16, 768)
    conv_lines = jnp.transpose(conv_state, (0, 2, 3, 1, 4)).reshape(2, 3, 2, 768)

    active, cum, size, more, *pieces = make_states(
        me,
        offsets,
        lengths,
        step_bias,
        decay_log,
        conv_input.reshape(2, 2, 256, 768),
        conv_lines,
        conv_weight.reshape(2, 4, 768),
        conv_bias,
        step_raw,
        init,
    )
    first = [passed_along(piece, 1) for piece in pieces[:3]]
    base = after(store_base, *pieces)
    bases = [base if n == 0 else passed_along(base, -n) for n in range(WINDOW)]
    plan = make_plan(me, hit_off, hit_at, store_offset.reshape(1, 512), bases)
    served, near = serve(me, plan, hit_off, hit_at, pieces, pool, pool_lines)
    down = passed_along(served, -1)
    mine, theirs = make_mixed(
        me,
        lengths,
        skip_weight,
        after(active, served),
        cum,
        size,
        init,
        gate_input,
        norm_gain,
        out_weight,
    )
    near = [near[:2], near[2:]]
    first, down, near, mine, theirs = lax.optimization_barrier((first, down, near, mine, theirs))

    second = passed_along(first[0], 1)
    two, one = passed_along(down, -1), passed_along(near[0], -1)
    other = lax.ppermute(theirs, "tp", [(i, i ^ 1) for i in range(8)])
    sums = [(mine[away].astype(F32) + other[away].astype(F32)).astype(BF16) for away in range(4)]

    def to_chip(away):
        return lax.ppermute(sums[away], "tp", [(i, (i + 2 * away) % 8) for i in range(8)])

    def if_needed(needed, part):
        return lax.cond(needed, lambda part: passed_along(part, 1), lambda part: part, part)

    def follow(parts):
        late = passed_along(parts[0], 1)
        return [late, passed_along(late, 1), passed_along(parts[1], 1)]

    parts = [to_chip(1), to_chip(3)]
    extra = lax.cond(
        more[0] > 0,
        follow,
        lambda parts: [parts[0], parts[0], parts[1]],
        [pieces[3], first[2]],
    )
    behind = if_needed(more[1] > 0, after(first[1], sums[0], extra[0], one))
    second, behind, two, one, parts, extra, sums, near = lax.optimization_barrier(
        (second, behind, two, one, parts, extra, sums, near)
    )

    third = passed_along(second[: THIRD[0]], 1)
    three, late = passed_along(two[: DOWN[2]], -1), passed_along(near[1], -1)
    terms = [sums[0], *parts, to_chip(2)]
    fourth = if_needed(more[2] > 0, second[THIRD[0] : THIRD[1]])
    layout = [(0, begin, end) for begin, end in zip(CUTS, CUTS[1:])]
    layout += [(1, begin, end) for begin, end in zip(CUTS[:3], CUTS[1:4])]
    layout += [(2, 0, 8), (2, 8, 12), (3, 0, THIRD[0]), (3, *THIRD)]
    layout += [(1, 14, 16), (2, 14, 16), (2, 12, 14)]
    pool_out, pool_lines_out, next_ssm, next_lines, mixed = settle(
        layout,
        me,
        plan,
        hit_off,
        hit_at,
        [*pieces, *first, second, behind, third, fourth, *extra],
        [one, late, two, three],
        pool,
        pool_lines,
        terms,
    )
    return (
        mixed.reshape(2, 2, 256, 256),
        pool_out.reshape(pool_ssm.shape),
        jnp.transpose(pool_lines_out.reshape(3, 1, 16, 768), (2, 0, 1, 3)),
        next_ssm.reshape(ssm_state.shape),
        jnp.transpose(next_lines.reshape(2, 3, 1, 2, 768), (0, 3, 1, 2, 4)),
    )


def solution(mesh):
    in_specs = (
        P(None, "cache", None, "tp", None),
        P(None, None, "tp", None),
        P(None, "tp", None),
        P(None, "cache", "tp", None),
        P(None, "tp"),
        P(None, "tp"),
        P(None, "tp"),
        P(None, "cache", None, "tp"),
        P(None, "tp"),
        P(None, "tp", None),
        P(None, "cache", "tp", None, None),
        P(None, "cache", None, "tp", None),
        P("cache", "tp", None, None),
        P("cache", None, "tp", None),
        P("cache"),
        P(),
        P("cache"),
        P(),
        P(),
    )
    out_specs = (
        P(None, "cache", None, "tp"),
        P("cache", "tp", None, None),
        P("cache", None, "tp", None),
        P(None, "cache", "tp", None, None),
        P(None, "cache", None, "tp", None),
    )
    return jax.shard_map(body, mesh=mesh, in_specs=in_specs, out_specs=out_specs, check_vma=False)
```
